256 devices in a mesh: grp: 8 (over x, core), dev: 32 (over z, y).
Axes of the slice: x: 4, y: 4, z: 8, core: 2. Of those that a mesh axis runs over, the one named last changes fastest.
Arguments:
- home_points: bfloat16 [524288, 512], P(('grp', 'dev')), may hold values from -6 to 6
- counts: int32 [256], P(('grp', 'dev')), may hold values from 0 to 2, as said below
- owner_group: int32 [512], P(('grp', 'dev')), may hold values from 0 to 7, as said below
- neighbors_home: int32 [27, 524288], P(None, ('grp', 'dev')), may hold values from 0 to 1023
- hilbert_target: int32 [4096], P(('grp', 'dev')), may hold values from 0 to 511, as said below
- neighbors_second: int32 [27, 262144], P(None, ('grp', 'dev')), may hold values from 0 to 1023
- depth_first: float32 [27, 512], replicated, may hold values from -1.5 to 1.5
- mixing_first: bfloat16 [512, 512], replicated, may hold values from -0.25 to 0.25
- gain_first: float32 [512], replicated, may hold values from 0.1 to 1.9
- w_qkv_first: bfloat16 [512, 1536], replicated, may hold values from -3 to 3
- w_out_first: bfloat16 [512, 512], replicated, may hold values from -0.25 to 0.25
- depth_second: float32 [27, 512], replicated, may hold values from -1.5 to 1.5
- mixing_second: bfloat16 [512, 512], replicated, may hold values from -0.25 to 0.25
- gain_second: float32 [512], replicated, may hold values from 0.1 to 1.9
- w_qkv_second: bfloat16 [512, 1536], replicated, may hold values from -3 to 3
- w_out_second: bfloat16 [512, 512], replicated, may hold values from -0.25 to 0.25
Outputs:
- encoded_points: bfloat16 [524288, 512], P(('grp', 'dev'))
The draws below stay inside these ranges and needn't reach their ends.
Inputs may be any that keep to these rules, and one draw needn't show every extreme that they name: For each dev index, the counts of its 8 tiles sum to 8. `owner_group`: the live slots of one tile name distinct groups, and for each dev index d and group q exactly one live slot of the tiles with dev index d names q. Dead slots' values are unused. `hilbert_target`: within each group the targets are a permutation of 0 to 511, and at most 2 blocks of one device name the same device (target // 16).
All inputs are finite; a program needn't handle non-finite values.
Results may differ from the reference program's by a relative error of at most 0.025.
Values may be sent and summed in bfloat16 or wider, within the bound.
No kernel may reach another device: no remote copies, remote signals or barrier semaphores. Data moves between devices by JAX's collectives and lax.ppermute only.
A program may use at most 128 MiB of HBM per device.

```python
import jax
import jax.numpy as jnp
from jax import lax

WIDTH = 512
HEADS = 8
HEAD_DIM = 64
PATCH = 1024
NEIGHBORS = 27
BLOCK = 64
BLOCKS = 16
SLOTS = 2
HOME_ROWS = 524288
OWNED_ROWS = 262144
N_GRP = 8
N_DEV = 32


def tile_plan(key):
    heavy_key, order_key, owner_key, spare_key = jax.random.split(key, 4)
    heavy = jax.random.randint(heavy_key, (N_DEV, 1), 1, N_GRP // 2 + 1)
    places = jnp.arange(N_GRP)[None, :]
    levels = jnp.where(places < heavy, SLOTS, jnp.where(places < 2 * heavy, 0, 1))
    shuffle = jnp.argsort(jax.random.randint(order_key, (N_DEV, N_GRP), 0, 1 << 20) * N_GRP + places, axis=1)
    tile_count = jnp.take_along_axis(levels, shuffle, axis=1)
    before = jnp.cumsum(tile_count, axis=1) - tile_count
    owner_perm = jnp.argsort(jax.random.randint(owner_key, (N_DEV, N_GRP), 0, 1 << 20) * N_GRP + places, axis=1)
    spots = jnp.minimum(before[:, :, None] + jnp.arange(SLOTS)[None, None, :], N_GRP - 1)
    chosen = jnp.take_along_axis(owner_perm, spots.reshape(N_DEV, N_GRP * SLOTS), axis=1)
    chosen = chosen.reshape(N_DEV, N_GRP, SLOTS)
    filled = jnp.arange(SLOTS)[None, None, :] < tile_count[:, :, None]
    spare = jax.random.randint(spare_key, (N_DEV, N_GRP, SLOTS), 0, N_GRP)
    owners = jnp.where(filled, chosen, spare)
    return (jnp.transpose(tile_count).reshape(-1).astype(jnp.int32), jnp.transpose(owners, (1, 0, 2)).reshape(-1).astype(jnp.int32))


def draw_counts(key, part):
    planned = tile_plan(key)
    return planned[0]


def draw_owner_group(key, part):
    planned = tile_plan(key)
    return planned[1]


def draw_hilbert_target(key, part):
    key = jax.random.fold_in(key, 5)

    def one_group(group):
        group_key = jax.random.fold_in(key, group)
        pool_key, shuffle_key, slot_key = jax.random.split(group_key, 3)
        candidates = jax.random.permutation(pool_key, 2 * N_DEV) % N_DEV
        leader = candidates[0]
        spots = jnp.arange(2 * N_DEV)
        ranked = jnp.argsort(jnp.where(candidates == leader, 2 * N_DEV + spots, spots))
        offsets = jnp.concatenate([jnp.stack([leader, leader]), candidates[ranked[:BLOCKS - 2]]])
        relabel = jax.random.permutation(shuffle_key, N_DEV)
        senders = jnp.arange(N_DEV)[:, None]
        destination = relabel[(senders + offsets[None, :]) % N_DEV]
        scores = jax.random.randint(slot_key, (N_DEV, BLOCKS), 0, 1 << 20) * BLOCKS + jnp.arange(BLOCKS)[None, :]
        layout = jnp.argsort(scores, axis=1)
        position = layout[destination, jnp.arange(BLOCKS)[None, :]]
        return destination * BLOCKS + position
    return jax.vmap(one_group)(jnp.arange(N_GRP)).reshape(-1).astype(jnp.int32)


def projection_draw(key):
    return (jax.random.normal(key, (WIDTH, 3 * WIDTH), jnp.float32) * 1.4 * WIDTH ** (-0.5)).astype(jnp.bfloat16)


def draw_w_qkv_first(key, part):
    key = jax.random.fold_in(key, 21)
    return projection_draw(key)


def draw_w_qkv_second(key, part):
    key = jax.random.fold_in(key, 37)
    return projection_draw(key)


def plant(array, rng, least, largest):
    extent = array.shape
    place = [jax.random.randint(jax.random.fold_in(rng, axis), (), 0, extent[axis]) for axis in range(len(extent))]
    array = array.at[tuple(place)].set(least)
    longest = extent.index(max(extent))
    place[longest] = (place[longest] + 1) % extent[longest]
    return array.at[tuple(place)].set(largest)


def shard_levels(key, extent, cuts, least, largest):
    def one(axis_at, parts):
        heights = jax.random.uniform(jax.random.fold_in(jax.random.fold_in(key, 6), axis_at), (parts,), jnp.float32, least / len(cuts), largest / len(cuts))
        return jnp.repeat(jnp.exp(heights), extent[axis_at] // parts).reshape((-1,) + (1,) * (len(extent) - axis_at - 1))

    loudness = one(*cuts[0])
    for cut in cuts[1:]:
        loudness = loudness * one(*cut)
    return loudness


def bell_draw(own_key, extent, width, reach, cuts=(), kind=jnp.bfloat16):
    entries = jax.random.normal(own_key, extent, jnp.float32) * width
    if len(cuts) > 0:
        entries = shard_levels(own_key, extent, cuts, -0.22, 0.18) * entries
    return jnp.clip(entries, min=-reach, max=reach).astype(kind)


def setup_inputs(seed: int = 0) -> dict:
    key_of = jax.random.split(jax.random.key(seed), 17)
    home_points = bell_draw(key_of[0], (HOME_ROWS, WIDTH), 1.0, 6.0, ((0, 256),))
    counts = draw_counts(jax.random.fold_in(key_of[16], 71), 0)
    owner_group = draw_owner_group(jax.random.fold_in(key_of[16], 71), 0)
    neighbors_home = plant(jax.random.randint(key_of[3], (NEIGHBORS, HOME_ROWS), 0, PATCH), jax.random.fold_in(key_of[3], 1), 0, PATCH - 1).astype(jnp.int32)
    hilbert_target = draw_hilbert_target(jax.random.fold_in(key_of[16], 71), 0)
    neighbors_second = plant(jax.random.randint(key_of[5], (NEIGHBORS, OWNED_ROWS), 0, PATCH), jax.random.fold_in(key_of[5], 1), 0, PATCH - 1).astype(jnp.int32)
    depth_first = bell_draw(key_of[6], (NEIGHBORS, WIDTH), 0.25, 1.5, (), jnp.float32)
    mixing_first = bell_draw(key_of[7], (WIDTH, WIDTH), WIDTH ** -0.5, 0.25)
    gain_first = jnp.clip(1.0 + 0.18 * jax.random.normal(key_of[8], (WIDTH,), jnp.float32), 0.1, 1.9)
    w_qkv_first = draw_w_qkv_first(jax.random.fold_in(key_of[16], 71), 0)
    w_out_first = bell_draw(key_of[10], (WIDTH, WIDTH), WIDTH ** -0.5, 0.25)
    depth_second = bell_draw(key_of[11], (NEIGHBORS, WIDTH), 0.25, 1.5, (), jnp.float32)
    mixing_second = bell_draw(key_of[12], (WIDTH, WIDTH), WIDTH ** -0.5, 0.25)
    gain_second = jnp.clip(1.0 + 0.18 * jax.random.normal(key_of[13], (WIDTH,), jnp.float32), 0.1, 1.9)
    w_qkv_second = draw_w_qkv_second(jax.random.fold_in(key_of[16], 71), 0)
    w_out_second = bell_draw(key_of[15], (WIDTH, WIDTH), WIDTH ** -0.5, 0.25)
    return dict(home_points=home_points, counts=counts, owner_group=owner_group, neighbors_home=neighbors_home, hilbert_target=hilbert_target, neighbors_second=neighbors_second, depth_first=depth_first, mixing_first=mixing_first, gain_first=gain_first, w_qkv_first=w_qkv_first, w_out_first=w_out_first, depth_second=depth_second, mixing_second=mixing_second, gain_second=gain_second, w_qkv_second=w_qkv_second, w_out_second=w_out_second)


epsilon = 1e-05

def encoder_block(features, neighbours, depth, mixing, gain, w_qkv, w_out):
    gathered = jnp.zeros(features.shape, jnp.float32)
    for which in range(NEIGHBORS):
        gathered = gathered + features[neighbours[which]].astype(jnp.float32) * depth[which]
    encoded = gathered.astype(jnp.bfloat16)
    updated = features.astype(jnp.float32) + jnp.dot(encoded, mixing, preferred_element_type=jnp.float32)
    centre = lax.optimization_barrier(jnp.mean(updated, axis=-1, keepdims=True))
    spread = lax.optimization_barrier(jnp.mean((updated - centre) ** 2, axis=-1, keepdims=True))
    normed = ((updated - centre) * lax.rsqrt(spread + epsilon) * gain).astype(jnp.bfloat16)
    project = jnp.dot(normed, w_qkv, preferred_element_type=jnp.float32).astype(jnp.bfloat16)
    pieces = project.astype(jnp.float32).reshape(PATCH, 3, HEADS, HEAD_DIM)
    scores = jnp.einsum('qhd,khd->hqk', pieces[:, 0], pieces[:, 1]) * HEAD_DIM ** (-0.5)
    peaks = lax.optimization_barrier(jnp.max(scores, axis=-1, keepdims=True))
    powers = jnp.exp(scores - peaks)
    totals = lax.optimization_barrier(jnp.sum(powers, axis=-1, keepdims=True))
    weights = (powers / totals).astype(jnp.bfloat16)
    mixed = jnp.einsum('hqk,khd->qhd', weights.astype(jnp.float32), pieces[:, 2])
    mixed = mixed.reshape(PATCH, WIDTH).astype(jnp.bfloat16)
    return (updated + jnp.dot(mixed, w_out, preferred_element_type=jnp.float32)).astype(jnp.bfloat16)

def reference(home_points, counts, owner_group, neighbors_home, hilbert_target, neighbors_second, depth_first, mixing_first, gain_first, w_qkv_first, w_out_first, depth_second, mixing_second, gain_second, w_qkv_second, w_out_second):
    groups = N_GRP
    owners = N_DEV
    points = home_points.reshape(groups, owners, SLOTS, PATCH, WIDTH)
    lists = neighbors_home.reshape(NEIGHBORS, groups, owners, SLOTS, PATCH)
    tile_count = counts.reshape(groups, owners)
    filled = jnp.arange(SLOTS, dtype=jnp.int32)[None, None, :] < tile_count[:, :, None]
    target = owner_group.reshape(groups, owners, SLOTS)
    match = filled[None] & (target[None] == jnp.arange(groups, dtype=jnp.int32)[:, None, None, None])
    labels = jnp.arange(groups, dtype=jnp.int32)[:, None, None] * SLOTS + jnp.arange(SLOTS, dtype=jnp.int32)[None, None, :]
    source = lax.optimization_barrier(jnp.sum(jnp.where(match, labels[None], 0), axis=(1, 3))).astype(jnp.int32)
    column = jnp.arange(owners, dtype=jnp.int32)[None, :]
    owned = points[source // SLOTS, column, source % SLOTS]
    owned_lists = jnp.transpose(lists[:, source // SLOTS, column, source % SLOTS], (1, 2, 0, 3))
    first_params = (depth_first, mixing_first, gain_first, w_qkv_first, w_out_first)
    second_params = (depth_second, mixing_second, gain_second, w_qkv_second, w_out_second)
    section_one = lax.map(lambda pair: encoder_block(pair[0], pair[1], *first_params), (owned.reshape(groups * owners, PATCH, WIDTH), owned_lists.reshape(groups * owners, NEIGHBORS, PATCH)))
    blocks_one = section_one.reshape(groups, owners * BLOCKS, BLOCK, WIDTH)
    order = hilbert_target.reshape(groups, owners * BLOCKS)
    rowsel = jnp.arange(groups, dtype=jnp.int32)[:, None]
    numbering = jnp.broadcast_to(jnp.arange(owners * BLOCKS, dtype=jnp.int32)[None, :], (groups, owners * BLOCKS))
    inverse = jnp.zeros((groups, owners * BLOCKS), jnp.int32).at[rowsel, order].set(numbering)
    regrouped = blocks_one[rowsel, inverse].reshape(groups * owners, PATCH, WIDTH)
    second_lists = jnp.transpose(neighbors_second.reshape(NEIGHBORS, groups * owners, PATCH), (1, 0, 2))
    section_two = lax.map(lambda pair: encoder_block(pair[0], pair[1], *second_params), (regrouped, second_lists))
    returned = section_two.reshape(groups, owners * BLOCKS, BLOCK, WIDTH)[rowsel, order]
    returned = returned.reshape(groups, owners, PATCH, WIDTH)
    homed = returned[target, jnp.arange(owners, dtype=jnp.int32)[None, :, None]]
    result = jnp.where(filled[:, :, :, None, None], homed, jnp.zeros((), jnp.bfloat16))
    return result.reshape(groups * owners * SLOTS * PATCH, WIDTH)
```

```python
import functools
import jax, jax.numpy as jnp
from jax import lax
from jax.experimental import pallas as pl
from jax.experimental.pallas import tpu as pltpu
from jax.sharding import PartitionSpec as P

HEADS = 8
HEAD_DIM = 64
epsilon = 1e-05
SCALE = HEAD_DIM ** (-0.5) * 1.4426950408889634
UNROLL = 8
TILE = 256


def block_kernel(arrives_split, lists, x_ref, depth_ref, mixing_ref, gain_ref, w_qkv_ref, w_out_ref, out_ref, plain, summed, updated, project, mixed):
    rows, width = x_ref.shape
    fanout = depth_ref.shape[0]
    lanes = 128
    chunks = width // lanes
    side = 32
    for c in range(chunks):
        cols = slice(c * lanes, (c + 1) * lanes)
        if arrives_split:
            for i in range(side):
                plain[pl.ds(i * chunks + c, side, stride=side * chunks), :] = x_ref[i * side : (i + 1) * side, cols].astype(jnp.float32)
        else:
            plain[pl.ds(c, rows, stride=chunks), :] = x_ref[:, cols].astype(jnp.float32)

    def gather(step, carry):
        first = step * UNROLL
        for u in range(UNROLL):
            total = None
            for j in range(fanout):
                start = lists[(first + u) * fanout + j]
                term = plain[pl.ds(start, chunks), :] * depth_ref[j]
                total = term if total is None else total + term
            summed[pl.ds(pl.multiple_of((first + u) * chunks, chunks), chunks), :] = total
        return carry

    lax.fori_loop(0, rows // UNROLL, gather, 0)

    def head(tile, carry):
        row0 = pl.multiple_of(tile * TILE, TILE)
        encoded = jnp.concatenate(
            [summed[pl.ds(row0 * chunks + c, TILE, stride=chunks), :] for c in range(chunks)], axis=1
        ).astype(jnp.bfloat16)
        groups = TILE // side
        residual = jnp.concatenate(
            [
                jnp.concatenate(
                    [plain[pl.ds((tile * groups + g) * chunks + c, side, stride=side * chunks), :] for g in range(groups)], axis=0
                )
                for c in range(chunks)
            ],
            axis=1,
        )
        up = residual + jnp.dot(encoded, mixing_ref[...], preferred_element_type=jnp.float32)
        updated[pl.ds(row0, TILE), :] = up
        centre = jnp.mean(up, axis=-1, keepdims=True)
        off = up - centre
        spread = jnp.mean(off * off, axis=-1, keepdims=True)
        normed = (off * lax.rsqrt(spread + epsilon) * gain_ref[...]).astype(jnp.bfloat16)
        project[pl.ds(row0, TILE), :width] = (
            jnp.dot(normed, w_qkv_ref[:, :width], preferred_element_type=jnp.float32) * SCALE
        ).astype(jnp.bfloat16)
        project[pl.ds(row0, TILE), width:] = jnp.dot(
            normed, w_qkv_ref[:, width:], preferred_element_type=jnp.float32
        ).astype(jnp.bfloat16)
        return carry

    lax.fori_loop(0, rows // TILE, head, 0)
    left = lax.broadcasted_iota(jnp.int32, (TILE, lanes), 1) < HEAD_DIM
    ones = jnp.ones((rows, lanes), jnp.bfloat16)
    for pair in range(width // lanes):
        cols = slice(pair * lanes, (pair + 1) * lanes)
        keys = project[:, width + pair * lanes : width + (pair + 1) * lanes]
        values = jnp.concatenate([project[:, 2 * width + pair * lanes : 2 * width + (pair + 1) * lanes], ones], axis=1)

        def attend(tile, carry):
            row0 = pl.multiple_of(tile * TILE, TILE)
            queries = project[pl.ds(row0, TILE), cols]
            results = []
            for half in range(2):
                keep = left if half == 0 else jnp.logical_not(left)
                own = jnp.where(keep, queries, jnp.zeros((), jnp.bfloat16))
                scores = lax.dot_general(own, keys, (((1,), (1,)), ((), ())), preferred_element_type=jnp.float32)
                peak = jnp.max(scores, axis=-1, keepdims=True)
                powers = jnp.exp2(scores - peak).astype(jnp.bfloat16)
                both = jnp.dot(powers, values, preferred_element_type=jnp.float32)
                results.append(both[:, :lanes] / both[:, lanes:])
            mixed[pl.ds(row0, TILE), cols] = jnp.where(left, results[0], results[1]).astype(jnp.bfloat16)
            return carry

        lax.fori_loop(0, rows // TILE, attend, 0)

    def tail(tile, carry):
        row0 = pl.multiple_of(tile * TILE, TILE)
        out_ref[pl.ds(row0, TILE), :] = (
            updated[pl.ds(row0, TILE), :]
            + jnp.dot(mixed[pl.ds(row0, TILE), :], w_out_ref[...], preferred_element_type=jnp.float32)
        ).astype(jnp.bfloat16)
        return carry

    lax.fori_loop(0, rows // TILE, tail, 0)


def encoder_block(features, lists, params, arrives_split):
    depth, mixing, gain, w_qkv, w_out = params
    rows, width = features.shape
    fanout = depth.shape[0]
    vmem = pl.BlockSpec(memory_space=pltpu.VMEM)
    return pl.pallas_call(
        functools.partial(block_kernel, arrives_split),
        out_shape=jax.ShapeDtypeStruct((rows, width), jnp.bfloat16),
        in_specs=[pl.BlockSpec(memory_space=pltpu.SMEM)] + [vmem] * 6,
        out_specs=vmem,
        scratch_shapes=[
            pltpu.VMEM((rows * 4, 128), jnp.float32),
            pltpu.VMEM((rows * 4, 128), jnp.float32),
            pltpu.VMEM((rows, width), jnp.float32),
            pltpu.VMEM((rows, 3 * width), jnp.bfloat16),
            pltpu.VMEM((rows, width), jnp.bfloat16),
        ],
        compiler_params=pltpu.CompilerParams(vmem_limit_bytes=48 << 20),
        cost_estimate=pl.CostEstimate(flops=5_000_000_000, bytes_accessed=6_000_000, transcendentals=8_000_000),
        name="block",
    )(lists, features, depth.reshape(fanout, 4, 128), mixing, gain.reshape(1, width), w_qkv, w_out)


def permute_kernel(x_ref, source_ref, out_ref):
    rows = x_ref.shape[0]
    positions = lax.broadcasted_iota(jnp.int32, (TILE, rows), 1)
    for tile in range(rows // TILE):
        own = slice(tile * TILE, (tile + 1) * TILE)
        chosen = jnp.where(positions == source_ref[own, :], 1.0, 0.0).astype(jnp.bfloat16)
        out_ref[own, :] = jnp.dot(chosen, x_ref[...], preferred_element_type=jnp.float32).astype(jnp.bfloat16)


def permute_rows(x, source):
    vmem = pl.BlockSpec(memory_space=pltpu.VMEM)
    return pl.pallas_call(
        permute_kernel,
        out_shape=jax.ShapeDtypeStruct(x.shape, x.dtype),
        in_specs=[vmem, vmem],
        out_specs=vmem,
        compiler_params=pltpu.CompilerParams(vmem_limit_bytes=32 << 20),
        cost_estimate=pl.CostEstimate(flops=1_100_000_000, bytes_accessed=2_100_000, transcendentals=0),
        name="permute",
    )(x, source.reshape(-1, 1))


def exchange(x, axis):
    return lax.all_to_all(x, axis, split_axis=0, concat_axis=0, tiled=True)


def body(
    home_points,
    counts,
    owner_group,
    neighbors_home,
    hilbert_target,
    neighbors_second,
    depth_first,
    mixing_first,
    gain_first,
    w_qkv_first,
    w_out_first,
    depth_second,
    mixing_second,
    gain_second,
    w_qkv_second,
    w_out_second,
):
    groups = lax.axis_size("grp")
    owners = lax.axis_size("dev")
    home_rows, width = home_points.shape
    slots = owner_group.shape[0]
    rows = home_rows // slots
    blocks = hilbert_target.shape[0]
    fanout = neighbors_home.shape[0]
    part = rows // groups
    side = rows // owners
    first_params = (depth_first, mixing_first, gain_first, w_qkv_first, w_out_first)
    second_params = (depth_second, mixing_second, gain_second, w_qkv_second, w_out_second)

    plan = lax.all_gather(jnp.concatenate([counts, owner_group]), "grp", axis=0, tiled=False)
    live = jnp.arange(slots)[None, :] < plan[:, :1]
    owner = plan[:, 1:].reshape(-1)
    live = live.reshape(-1)
    match = live[None, :] & (owner[None, :] == jnp.arange(groups)[:, None])
    source = jnp.sum(jnp.where(match, jnp.arange(groups * slots)[None, :], 0), axis=1)
    target = lax.all_gather(hilbert_target, "dev", axis=0, tiled=True)
    pieces = target.shape[0]
    inverse = jnp.sum(
        jnp.where(target[None, :] == jnp.arange(pieces)[:, None], jnp.arange(pieces)[None, :], 0), axis=1
    )
    pair = jnp.arange(2)[None, :]
    forward_rows = (2 * inverse[:, None] + pair).reshape(-1)
    backward_rows = (2 * target[:, None] + pair).reshape(-1)

    def ordered(lists):
        return jnp.transpose(lists.reshape(fanout, -1, owners, owners), (1, 3, 2, 0))

    home_lists = ordered(neighbors_home).reshape(slots, 2, -1)
    packed = home_lists[:, 0] + home_lists[:, 1] * 65536
    packed = jnp.transpose(packed.reshape(slots, groups, -1), (1, 0, 2))
    second_lists = ordered(neighbors_second).reshape(-1) * 4

    points = jnp.transpose(home_points.reshape(slots, groups, part, width), (1, 0, 2, 3))
    spread = exchange(points, "grp").reshape(groups * slots, part, width)
    spread_lists = exchange(packed, "grp").reshape(groups * slots, -1)
    owned = exchange(spread[source], "grp").reshape(rows, width)
    owned_lists = exchange(spread_lists[source], "grp").reshape(-1)
    first_lists = jnp.concatenate([owned_lists & 65535, owned_lists >> 16]) * 4

    section_one = encoder_block(owned, first_lists, first_params, False)
    mid = exchange(section_one.reshape(owners, side, width), "dev").reshape(rows, width)
    mid = permute_rows(mid, forward_rows)
    regrouped = exchange(mid.reshape(owners, side, width), "dev").reshape(rows, width)
    section_two = encoder_block(regrouped, second_lists, second_params, True)
    mid = exchange(section_two.reshape(owners, side, width), "dev").reshape(rows, width)
    mid = permute_rows(mid, backward_rows)
    returned = exchange(mid.reshape(owners, side, width), "dev").reshape(groups, part, width)
    gathered = exchange(returned, "grp")
    homeward = jnp.where(live[:, None, None], gathered[owner], jnp.zeros((), jnp.bfloat16))
    delivered = exchange(homeward.reshape(groups, slots, part, width), "grp")
    result = delivered.reshape(groups, slots, owners // groups, side, width)
    return jnp.transpose(result, (1, 3, 0, 2, 4)).reshape(home_rows, width)


def solution(mesh):
    return jax.shard_map(
        body,
        mesh=mesh,
        in_specs=(
            P(("grp", "dev"), None),
            P(("grp", "dev")),
            P(("grp", "dev")),
            P(None, ("grp", "dev")),
            P(("grp", "dev")),
            P(None, ("grp", "dev")),
            P(),
            P(),
            P(),
            P(),
            P(),
            P(),
            P(),
            P(),
            P(),
            P(),
        ),
        out_specs=P(("grp", "dev"), None),
        check_vma=False,
    )
```

```python
import functools
import jax
import jax.numpy as jnp
from jax import lax
from jax.experimental import pallas as pl
from jax.experimental.pallas import tpu as pltpu
from jax.sharding import PartitionSpec as P

HEADS = 8
HEAD_DIM = 64
epsilon = 1e-05
SCALE = HEAD_DIM ** (-0.5) * 1.4426950408889634
LANES = 128
TILE = 256
SIDE = 32
CHUNK = 128
BUFFERS = 2
LIST_ROWS = 14


def block_kernel(first, *refs):
    if first:
        (
            x_ref, depth_ref, mixing_ref, gain_ref, w_qkv_ref, w_out_ref, out_ref,
            plain, summed, updated, project, mixed, scores_even, scores_odd, lists_ref, *stage
        ) = refs
    else:
        (
            lists_ref, x_ref, depth_ref, mixing_ref, gain_ref, w_qkv_ref, w_out_ref, out_ref,
            plain, summed, updated, project, mixed, scores_even, scores_odd, *stage
        ) = refs
    buffers, sems = stage[:BUFFERS], stage[BUFFERS]
    rows, width = out_ref.shape
    fanout = depth_ref.shape[0]
    chunks = width // LANES
    pairs = width // LANES
    tiles = rows // TILE
    count = rows // CHUNK
    if first:
        parts = x_ref.shape[0]
        part = rows // parts
        halves = parts // 4

        def digits(block):
            upper = x_ref[2 * block, part : part + LIST_ROWS, :]
            lower = x_ref[2 * block + 1, part : part + LIST_ROWS, :]
            return upper.astype(jnp.float32), lower.astype(jnp.float32)

        for half in range(halves):
            high, low = digits(half), digits(halves + half)
            for piece in range(2):
                found = ((high[piece] * 32.0 + low[piece]) * chunks).astype(jnp.int32)
                kept = min(LIST_ROWS, fanout - piece * LIST_ROWS)
                for c in range(chunks):
                    lists_ref[half * chunks + c, piece * LIST_ROWS : piece * LIST_ROWS + kept, :] = found[
                        :kept, c * LANES : (c + 1) * LANES
                    ]

    def fetch(chunk, slot):
        return pltpu.make_async_copy(lists_ref.at[chunk], buffers[slot], sems.at[slot])

    for slot in range(BUFFERS):
        fetch(slot, slot).start()
    for c in range(chunks):
        cols = slice(c * LANES, (c + 1) * LANES)
        if first:
            for p in range(parts):
                plain[pl.ds(p * part * chunks + c, part, stride=chunks), :] = x_ref[p, :part, cols].astype(jnp.float32)
        else:
            plain[pl.ds(c, rows, stride=chunks), :] = x_ref[:, cols].astype(jnp.float32)

    def gather(step, carry):
        for slot in range(BUFFERS):
            chunk = step * BUFFERS + slot
            fetch(chunk, slot).wait()
            base = pl.multiple_of(chunk * (CHUNK // SIDE) * chunks, (CHUNK // SIDE) * chunks)
            for u in range(CHUNK):
                total = None
                for j in range(fanout):
                    term = plain[pl.ds(buffers[slot][j, u], chunks), :] * depth_ref[j]
                    total = term if total is None else total + term
                summed[pl.ds(base + ((u % SIDE) * SIDE + u // SIDE) * chunks, chunks), :] = total

            @pl.when(chunk + BUFFERS < count)
            def _():
                fetch(chunk + BUFFERS, slot).start()

        return carry

    lax.fori_loop(0, count // BUFFERS, gather, 0)

    def head(tile, carry):
        row0 = pl.multiple_of(tile * TILE, TILE)
        encoded = jnp.concatenate(
            [summed[pl.ds(row0 * chunks + c, TILE, stride=chunks), :] for c in range(chunks)], axis=1
        ).astype(jnp.bfloat16)
        if first:
            groups = TILE // SIDE
            residual = jnp.concatenate(
                [
                    jnp.concatenate(
                        [
                            plain[pl.ds((tile * groups + g) * chunks + c, SIDE, stride=SIDE * chunks), :]
                            for g in range(groups)
                        ],
                        axis=0,
                    )
                    for c in range(chunks)
                ],
                axis=1,
            )
        else:
            residual = x_ref[pl.ds(row0, TILE), :].astype(jnp.float32)
        up = residual + jnp.dot(encoded, mixing_ref[...], preferred_element_type=jnp.float32)
        updated[pl.ds(row0, TILE), :] = up
        centre = jnp.mean(up, axis=-1, keepdims=True)
        off = up - centre
        spread = jnp.mean(off * off, axis=-1, keepdims=True)
        normed = (off * lax.rsqrt(spread + epsilon) * gain_ref[...]).astype(jnp.bfloat16)
        project[pl.ds(row0, TILE), :width] = (
            jnp.dot(normed, w_qkv_ref[:, :width], preferred_element_type=jnp.float32) * SCALE
        ).astype(jnp.bfloat16)
        project[pl.ds(row0, TILE), width:] = jnp.dot(
            normed, w_qkv_ref[:, width:], preferred_element_type=jnp.float32
        ).astype(jnp.bfloat16)
        return carry

    lax.fori_loop(0, tiles, head, 0)
    left = lax.broadcasted_iota(jnp.int32, (TILE, LANES), 1) < HEAD_DIM
    ones = jnp.ones((rows, LANES), jnp.bfloat16)

    def place(step):
        row0 = pl.multiple_of(lax.rem(step, tiles) * TILE, TILE)
        col0 = pl.multiple_of(lax.div(step, tiles) * LANES, LANES)
        return row0, col0

    def score(step, half, target):
        row0, col0 = place(step)
        queries = project[pl.ds(row0, TILE), pl.ds(col0, LANES)]
        keep = left if half == 0 else jnp.logical_not(left)
        own = jnp.where(keep, queries, jnp.zeros((), jnp.bfloat16))
        keys = project[:, pl.ds(width + col0, LANES)]
        target[...] = lax.dot_general(own, keys, (((1,), (1,)), ((), ())), preferred_element_type=jnp.float32)

    def weigh(step, source):
        row0, col0 = place(step)
        scores = source[...]
        values = jnp.concatenate([project[:, pl.ds(2 * width + col0, LANES)], ones], axis=1)
        peak = jnp.max(scores, axis=-1, keepdims=True)
        powers = jnp.exp2(scores - peak).astype(jnp.bfloat16)
        both = jnp.dot(powers, values, preferred_element_type=jnp.float32)
        return both[:, :LANES] / both[:, LANES:]

    score(0, 0, scores_even)

    def attend(step, carry):
        row0, col0 = place(step)
        score(step, 1, scores_odd)
        left_result = weigh(step, scores_even)
        score(jnp.minimum(step + 1, pairs * tiles - 1), 0, scores_even)
        right_result = weigh(step, scores_odd)
        mixed[pl.ds(row0, TILE), pl.ds(col0, LANES)] = jnp.where(left, left_result, right_result).astype(jnp.bfloat16)
        return carry

    lax.fori_loop(0, pairs * tiles, attend, 0)

    def tail(tile, carry):
        row0 = pl.multiple_of(tile * TILE, TILE)
        out_ref[pl.ds(row0, TILE), :] = (
            updated[pl.ds(row0, TILE), :]
            + jnp.dot(mixed[pl.ds(row0, TILE), :], w_out_ref[...], preferred_element_type=jnp.float32)
        ).astype(jnp.bfloat16)
        return carry

    lax.fori_loop(0, tiles, tail, 0)


def encoder_block(features, lists, params, rows):
    depth, mixing, gain, w_qkv, w_out = params
    fanout, width = depth.shape
    first = lists is None
    vmem = pl.BlockSpec(memory_space=pltpu.VMEM)
    table = (rows // CHUNK, SIDE, LANES)
    operands = (features, depth.reshape(fanout, -1, LANES), mixing, gain.reshape(1, width), w_qkv, w_out)
    if not first:
        operands = (lists,) + operands
    return pl.pallas_call(
        functools.partial(block_kernel, first),
        out_shape=jax.ShapeDtypeStruct((rows, width), jnp.bfloat16),
        in_specs=[vmem] * len(operands),
        out_specs=vmem,
        scratch_shapes=[
            pltpu.VMEM((rows * 4, LANES), jnp.float32),
            pltpu.VMEM((rows * 4, LANES), jnp.float32),
            pltpu.VMEM((rows, width), jnp.float32),
            pltpu.VMEM((rows, 3 * width), jnp.bfloat16),
            pltpu.VMEM((rows, width), jnp.bfloat16),
            pltpu.VMEM((TILE, rows), jnp.float32),
            pltpu.VMEM((TILE, rows), jnp.float32),
        ]
        + [pltpu.VMEM(table, jnp.int32)] * first
        + [pltpu.SMEM(table[1:], jnp.int32)] * BUFFERS
        + [pltpu.SemaphoreType.DMA((BUFFERS,))],
        compiler_params=pltpu.CompilerParams(vmem_limit_bytes=48 << 20),
        cost_estimate=pl.CostEstimate(flops=5_000_000_000, bytes_accessed=6_000_000, transcendentals=8_000_000),
        name="block",
    )(*operands)


def staged(lists, rows):
    fanout = lists.shape[0]
    table = jnp.transpose((lists * 4).reshape(fanout, rows // CHUNK, LANES), (1, 0, 2))
    return jnp.pad(table, ((0, 0), (0, SIDE - fanout), (0, 0)))


def enclosed(neighbors, plan, slots, groups, width):
    fanout = neighbors.shape[0]
    lists = jnp.transpose(neighbors.reshape(fanout, slots, -1, width), (1, 2, 0, 3))
    lists = jnp.pad(lists, ((0, 0), (0, 0), (0, 2 * LIST_ROWS - fanout), (0, 0)))
    letters = jnp.concatenate([lists // 32, lists % 32], axis=1).reshape(slots, groups, LIST_ROWS, width)
    note = jnp.broadcast_to(jnp.pad(plan, (0, width - plan.shape[0])), (slots, groups, 2, width))
    return jnp.concatenate([letters, note], axis=2).astype(jnp.bfloat16)


def permute_kernel(x_ref, source_ref, out_ref):
    rows = x_ref.shape[0]
    positions = lax.broadcasted_iota(jnp.int32, (TILE, rows), 1)
    for tile in range(rows // TILE):
        own = slice(tile * TILE, (tile + 1) * TILE)
        chosen = jnp.where(positions == source_ref[own, :], 1.0, 0.0).astype(jnp.bfloat16)
        out_ref[own, :] = jnp.dot(chosen, x_ref[...], preferred_element_type=jnp.float32).astype(jnp.bfloat16)


def permute_rows(x, source):
    vmem = pl.BlockSpec(memory_space=pltpu.VMEM)
    return pl.pallas_call(
        permute_kernel,
        out_shape=jax.ShapeDtypeStruct(x.shape, x.dtype),
        in_specs=[vmem, vmem],
        out_specs=vmem,
        compiler_params=pltpu.CompilerParams(vmem_limit_bytes=32 << 20),
        cost_estimate=pl.CostEstimate(flops=1_100_000_000, bytes_accessed=2_100_000, transcendentals=0),
        name="permute",
    )(x, source.reshape(-1, 1))


def pick_kernel(source_ref, x_ref, out_ref, sems):
    copies = [
        pltpu.make_async_copy(x_ref.at[source_ref[q]], out_ref.at[q], sems.at[q]) for q in range(out_ref.shape[0])
    ]
    for copy in copies:
        copy.start()
    for copy in copies:
        copy.wait()


def pick_parts(x, source):
    count = source.shape[0]
    return pl.pallas_call(
        pick_kernel,
        out_shape=jax.ShapeDtypeStruct((count,) + x.shape[1:], x.dtype),
        in_specs=[pl.BlockSpec(memory_space=pltpu.SMEM), pl.BlockSpec(memory_space=pl.ANY)],
        out_specs=pl.BlockSpec(memory_space=pltpu.VMEM),
        scratch_shapes=[pltpu.SemaphoreType.DMA((count,))],
        compiler_params=pltpu.CompilerParams(vmem_limit_bytes=32 << 20),
        cost_estimate=pl.CostEstimate(flops=0, bytes_accessed=2_100_000, transcendentals=0),
        name="pick",
    )(source, x)


def homeward_kernel(owner_ref, live_ref, x_ref, out_ref):
    groups, slots, part, width = out_ref.shape
    quarter = part // SIDE
    row = lax.broadcasted_iota(jnp.int32, (part, part), 0)
    column = lax.broadcasted_iota(jnp.int32, (part, part), 1)
    order = jnp.where(column == (row % SIDE) * quarter + row // SIDE, 1.0, 0.0).astype(jnp.bfloat16)
    for g in range(groups):
        for s in range(slots):
            start = pl.multiple_of(owner_ref[g * slots + s] * part, part)
            piece = jnp.dot(order, x_ref[pl.ds(start, part), :], preferred_element_type=jnp.float32)
            keep = live_ref[g * slots + s] > 0
            out_ref[g, s] = jnp.where(keep, piece, 0.0).astype(jnp.bfloat16)


def homeward_parts(x, owner, live, groups, slots):
    rows, width = x.shape
    smem = pl.BlockSpec(memory_space=pltpu.SMEM)
    vmem = pl.BlockSpec(memory_space=pltpu.VMEM)
    return pl.pallas_call(
        homeward_kernel,
        out_shape=jax.ShapeDtypeStruct((groups, slots, rows // groups, width), x.dtype),
        in_specs=[smem, smem, vmem],
        out_specs=vmem,
        compiler_params=pltpu.CompilerParams(vmem_limit_bytes=32 << 20),
        cost_estimate=pl.CostEstimate(flops=270_000_000, bytes_accessed=3_200_000, transcendentals=0),
        name="homeward",
    )(owner, live, x)


def exchange(x, axis):
    return lax.all_to_all(x, axis, split_axis=0, concat_axis=0, tiled=True)


def body(
    home_points,
    counts,
    owner_group,
    neighbors_home,
    hilbert_target,
    neighbors_second,
    depth_first,
    mixing_first,
    gain_first,
    w_qkv_first,
    w_out_first,
    depth_second,
    mixing_second,
    gain_second,
    w_qkv_second,
    w_out_second,
):
    groups = lax.axis_size("grp")
    owners = lax.axis_size("dev")
    home_rows, width = home_points.shape
    slots = owner_group.shape[0]
    rows = home_rows // slots
    blocks = hilbert_target.shape[0]
    part = rows // groups
    side = rows // owners
    first_params = (depth_first, mixing_first, gain_first, w_qkv_first, w_out_first)
    second_params = (depth_second, mixing_second, gain_second, w_qkv_second, w_out_second)

    letters = enclosed(neighbors_home, jnp.concatenate([counts, owner_group]), slots, groups, width)
    points = jnp.concatenate([home_points.reshape(slots, groups, part, width), letters], axis=2)
    spread = exchange(jnp.transpose(points, (1, 0, 2, 3)), "grp")
    plan = spread[:, 0, part + LIST_ROWS, : 1 + slots].astype(jnp.int32)
    live = (jnp.arange(slots)[None, :] < plan[:, :1]).reshape(-1)
    owner = plan[:, 1:].reshape(-1)
    match = live[None, :] & (owner[None, :] == jnp.arange(groups)[:, None])
    source = jnp.sum(jnp.where(match, jnp.arange(groups * slots)[None, :], 0), axis=1)
    owned = exchange(pick_parts(spread.reshape((groups * slots,) + spread.shape[2:]), source), "grp")

    arrival = (neighbors_second % side) * side + neighbors_second // side
    second_lists = staged(arrival, rows)
    owned, hilbert_target = lax.optimization_barrier((owned, hilbert_target))
    targets = exchange(jnp.broadcast_to(hilbert_target[None], (owners, blocks)), "dev")
    section_one = encoder_block(owned, None, first_params, rows)
    flat = targets.reshape(-1)
    pieces = flat.shape[0]
    inverse = jnp.sum(jnp.where(flat[None, :] == jnp.arange(pieces)[:, None], jnp.arange(pieces)[None, :], 0), axis=1)
    pair = jnp.arange(2)[None, :]
    forward_rows = (2 * inverse[:, None] + pair).reshape(-1)
    by_part = jnp.transpose(targets.reshape(owners, groups, -1), (1, 0, 2)).reshape(-1, 1)
    backward_rows = (2 * by_part + pair).reshape(-1)

    mid = exchange(section_one.reshape(owners, side, width), "dev").reshape(rows, width)
    mid = permute_rows(mid, forward_rows)
    regrouped = exchange(mid.reshape(owners, side, width), "dev").reshape(rows, width)
    section_two = encoder_block(regrouped, second_lists, second_params, rows)
    mid = exchange(section_two.reshape(owners, side, width), "dev").reshape(rows, width)
    mid = permute_rows(mid, backward_rows)
    returned = exchange(mid.reshape(groups * owners, -1, width), ("grp", "dev")).reshape(rows, width)
    homeward = homeward_parts(returned, owner, live.astype(jnp.int32), groups, slots)
    delivered = exchange(homeward, "grp")
    return jnp.transpose(delivered, (1, 0, 2, 3)).reshape(home_rows, width)


def solution(mesh):
    return jax.shard_map(
        body,
        mesh=mesh,
        in_specs=(
            P(("grp", "dev"), None),
            P(("grp", "dev")),
            P(("grp", "dev")),
            P(None, ("grp", "dev")),
            P(("grp", "dev")),
            P(None, ("grp", "dev")),
            P(),
            P(),
            P(),
            P(),
            P(),
            P(),
            P(),
            P(),
            P(),
            P(),
        ),
        out_specs=P(("grp", "dev"), None),
        check_vma=False,
    )
```

```python
import functools
import jax
import jax.numpy as jnp
from jax import lax
from jax.experimental import pallas as pl
from jax.experimental.pallas import tpu as pltpu
from jax.sharding import PartitionSpec as P

HEADS = 8
HEAD_DIM = 64
epsilon = 1e-05
SCALE = HEAD_DIM ** (-0.5) * 1.4426950408889634
LANES = 128
TILE = 256
SIDE = 32
CHUNK = 128
BUFFERS = 2
LIST_ROWS = 14
NOTE_ROWS = 8


def block_kernel(first, *refs):
    if first:
        (
            x_ref, note_ref, depth_ref, mixing_ref, gain_ref, w_qkv_ref, w_out_ref, out_ref,
            plain, summed, updated, project, mixed, scores_even, scores_odd, powers_even, powers_odd, lists_ref, *stage
        ) = refs
    else:
        (
            lists_ref, x_ref, depth_ref, mixing_ref, gain_ref, w_qkv_ref, w_out_ref, out_ref,
            plain, summed, updated, project, mixed, scores_even, scores_odd, powers_even, powers_odd, *stage
        ) = refs
    buffers, sems = stage[:BUFFERS], stage[BUFFERS]
    rows, width = updated.shape
    fanout = depth_ref.shape[0]
    chunks = width // LANES
    pairs = width // LANES
    tiles = rows // TILE
    count = rows // CHUNK
    if first:
        parts = x_ref.shape[0]
        part = rows // parts
        halves = parts // 4

        def digits(block):
            upper = x_ref[2 * block, part : part + LIST_ROWS, :]
            lower = x_ref[2 * block + 1, part : part + LIST_ROWS, :]
            return upper.astype(jnp.float32), lower.astype(jnp.float32)

        for half in range(halves):
            high, low = digits(half), digits(halves + half)
            for piece in range(2):
                found = ((high[piece] * 32.0 + low[piece]) * chunks).astype(jnp.int32)
                kept = min(LIST_ROWS, fanout - piece * LIST_ROWS)
                for c in range(chunks):
                    lists_ref[half * chunks + c, piece * LIST_ROWS : piece * LIST_ROWS + kept, :] = found[
                        :kept, c * LANES : (c + 1) * LANES
                    ]

    def fetch(chunk, slot):
        return pltpu.make_async_copy(lists_ref.at[chunk], buffers[slot], sems.at[slot])

    for slot in range(BUFFERS):
        fetch(slot, slot).start()
    for c in range(chunks):
        cols = slice(c * LANES, (c + 1) * LANES)
        if first:
            for p in range(parts):
                plain[pl.ds(p * part * chunks + c, part, stride=chunks), :] = x_ref[p, :part, cols].astype(jnp.float32)
        else:
            plain[pl.ds(c, rows, stride=chunks), :] = x_ref[:, cols].astype(jnp.float32)

    def gather(step, carry):
        for slot in range(BUFFERS):
            chunk = step * BUFFERS + slot
            fetch(chunk, slot).wait()
            base = pl.multiple_of(chunk * (CHUNK // SIDE) * chunks, (CHUNK // SIDE) * chunks)
            for u in range(CHUNK):
                total = None
                for j in range(fanout):
                    term = plain[pl.ds(buffers[slot][j, u], chunks), :] * depth_ref[j]
                    total = term if total is None else total + term
                summed[pl.ds(base + ((u % SIDE) * SIDE + u // SIDE) * chunks, chunks), :] = total

            @pl.when(chunk + BUFFERS < count)
            def _():
                fetch(chunk + BUFFERS, slot).start()

        return carry

    lax.fori_loop(0, count // BUFFERS, gather, 0)

    def head(tile, carry):
        row0 = pl.multiple_of(tile * TILE, TILE)
        encoded = jnp.concatenate(
            [summed[pl.ds(row0 * chunks + c, TILE, stride=chunks), :] for c in range(chunks)], axis=1
        ).astype(jnp.bfloat16)
        if first:
            groups = TILE // SIDE
            residual = jnp.concatenate(
                [
                    jnp.concatenate(
                        [
                            plain[pl.ds((tile * groups + g) * chunks + c, SIDE, stride=SIDE * chunks), :]
                            for g in range(groups)
                        ],
                        axis=0,
                    )
                    for c in range(chunks)
                ],
                axis=1,
            )
        else:
            residual = x_ref[pl.ds(row0, TILE), :].astype(jnp.float32)
        up = residual + jnp.dot(encoded, mixing_ref[...], preferred_element_type=jnp.float32)
        updated[pl.ds(row0, TILE), :] = up
        centre = jnp.mean(up, axis=-1, keepdims=True)
        off = up - centre
        spread = jnp.mean(off * off, axis=-1, keepdims=True)
        normed = (off * lax.rsqrt(spread + epsilon) * gain_ref[...]).astype(jnp.bfloat16)
        project[pl.ds(row0, TILE), :width] = (
            jnp.dot(normed, w_qkv_ref[:, :width], preferred_element_type=jnp.float32) * SCALE
        ).astype(jnp.bfloat16)
        project[pl.ds(row0, TILE), width:] = jnp.dot(
            normed, w_qkv_ref[:, width:], preferred_element_type=jnp.float32
        ).astype(jnp.bfloat16)
        return carry

    lax.fori_loop(0, tiles, head, 0)
    left = lax.broadcasted_iota(jnp.int32, (TILE, LANES), 1) < HEAD_DIM
    ones = jnp.ones((rows, LANES), jnp.bfloat16)

    def place(step):
        row0 = pl.multiple_of(lax.rem(step, tiles) * TILE, TILE)
        col0 = pl.multiple_of(lax.div(step, tiles) * LANES, LANES)
        return row0, col0

    def score(step, half, target):
        row0, col0 = place(step)
        queries = project[pl.ds(row0, TILE), pl.ds(col0, LANES)]
        keep = left if half == 0 else jnp.logical_not(left)
        own = jnp.where(keep, queries, jnp.zeros((), jnp.bfloat16))
        keys = project[:, pl.ds(width + col0, LANES)]
        target[...] = lax.dot_general(own, keys, (((1,), (1,)), ((), ())), preferred_element_type=jnp.float32)

    def weigh(source, target):
        scores = source[...]
        peak = jnp.max(scores, axis=-1, keepdims=True)
        target[...] = jnp.exp2(scores - peak).astype(jnp.bfloat16)

    def blend(step, half, source):
        row0, col0 = place(step)
        values = jnp.concatenate([project[:, pl.ds(2 * width + col0, LANES)], ones], axis=1)
        both = jnp.dot(source[...], values, preferred_element_type=jnp.float32)
        result = (both[:, :LANES] / both[:, LANES:]).astype(jnp.bfloat16)
        keep = left if half == 0 else jnp.logical_not(left)
        spot = (pl.ds(row0, TILE), pl.ds(col0, LANES))
        mixed[spot] = jnp.where(keep, result, mixed[spot])

    last = pairs * tiles - 1
    score(0, 0, scores_even)
    powers_odd[...] = jnp.ones_like(powers_odd)

    def attend(step, carry):
        score(step, 1, scores_odd)
        weigh(scores_even, powers_even)
        blend(jnp.maximum(step - 1, 0), 1, powers_odd)
        score(jnp.minimum(step + 1, last), 0, scores_even)
        weigh(scores_odd, powers_odd)
        blend(step, 0, powers_even)
        return carry

    lax.fori_loop(0, pairs * tiles, attend, 0)
    blend(last, 1, powers_odd)

    def tail(tile, carry):
        row0 = pl.multiple_of(tile * TILE, TILE)
        result = (
            updated[pl.ds(row0, TILE), :]
            + jnp.dot(mixed[pl.ds(row0, TILE), :], w_out_ref[...], preferred_element_type=jnp.float32)
        ).astype(jnp.bfloat16)
        if first:
            for i in range(TILE // SIDE):
                for c in range(chunks):
                    out_ref[tile * (TILE // SIDE) + i, c * SIDE : (c + 1) * SIDE, :] = result[
                        i * SIDE : (i + 1) * SIDE, c * LANES : (c + 1) * LANES
                    ]
        else:
            out_ref[pl.ds(row0, TILE), :] = result
        return carry

    lax.fori_loop(0, tiles, tail, 0)
    if first:
        for i in range(rows // SIDE):
            out_ref[i, chunks * SIDE :, :] = note_ref[...]


def encoder_block(features, beside, params, rows, first):
    depth, mixing, gain, w_qkv, w_out = params
    fanout, width = depth.shape
    vmem = pl.BlockSpec(memory_space=pltpu.VMEM)
    table = (rows // CHUNK, SIDE, LANES)
    operands = (depth.reshape(fanout, -1, LANES), mixing, gain.reshape(1, width), w_qkv, w_out)
    operands = ((features, beside) if first else (beside, features)) + operands
    shape = (rows // SIDE, SIDE * width // LANES + NOTE_ROWS, LANES) if first else (rows, width)
    return pl.pallas_call(
        functools.partial(block_kernel, first),
        out_shape=jax.ShapeDtypeStruct(shape, jnp.bfloat16),
        in_specs=[vmem] * len(operands),
        out_specs=vmem,
        scratch_shapes=[
            pltpu.VMEM((rows * 4, LANES), jnp.float32),
            pltpu.VMEM((rows * 4, LANES), jnp.float32),
            pltpu.VMEM((rows, width), jnp.float32),
            pltpu.VMEM((rows, 3 * width), jnp.bfloat16),
            pltpu.VMEM((rows, width), jnp.bfloat16),
            pltpu.VMEM((TILE, rows), jnp.float32),
            pltpu.VMEM((TILE, rows), jnp.float32),
            pltpu.VMEM((TILE, rows), jnp.bfloat16),
            pltpu.VMEM((TILE, rows), jnp.bfloat16),
        ]
        + [pltpu.VMEM(table, jnp.int32)] * first
        + [pltpu.SMEM(table[1:], jnp.int32)] * BUFFERS
        + [pltpu.SemaphoreType.DMA((BUFFERS,))],
        compiler_params=pltpu.CompilerParams(vmem_limit_bytes=48 << 20),
        cost_estimate=pl.CostEstimate(flops=5_000_000_000, bytes_accessed=6_000_000, transcendentals=8_000_000),
        name="block",
    )(*operands)


def staged(lists, rows):
    fanout = lists.shape[0]
    table = jnp.transpose((lists * 4).reshape(fanout, rows // CHUNK, LANES), (1, 0, 2))
    return jnp.pad(table, ((0, 0), (0, SIDE - fanout), (0, 0)))


def enclosed(neighbors, plan, slots, groups, width):
    fanout = neighbors.shape[0]
    lists = jnp.transpose(neighbors.reshape(fanout, slots, -1, width), (1, 2, 0, 3))
    lists = jnp.pad(lists, ((0, 0), (0, 0), (0, 2 * LIST_ROWS - fanout), (0, 0)))
    letters = jnp.concatenate([lists // 32, lists % 32], axis=1).reshape(slots, groups, LIST_ROWS, width)
    note = jnp.broadcast_to(jnp.pad(plan, (0, width - plan.shape[0])), (slots, groups, 2, width))
    return jnp.concatenate([letters, note], axis=2).astype(jnp.bfloat16)


def permute_kernel(x_ref, source_ref, out_ref):
    rows = x_ref.shape[0]
    positions = lax.broadcasted_iota(jnp.int32, (TILE, rows), 1)
    for tile in range(rows // TILE):
        own = slice(tile * TILE, (tile + 1) * TILE)
        chosen = jnp.where(positions == source_ref[own, :], 1.0, 0.0).astype(jnp.bfloat16)
        out_ref[own, :] = jnp.dot(chosen, x_ref[...], preferred_element_type=jnp.float32).astype(jnp.bfloat16)


def permute_rows(x, source):
    vmem = pl.BlockSpec(memory_space=pltpu.VMEM)
    return pl.pallas_call(
        permute_kernel,
        out_shape=jax.ShapeDtypeStruct(x.shape, x.dtype),
        in_specs=[vmem, vmem],
        out_specs=vmem,
        compiler_params=pltpu.CompilerParams(vmem_limit_bytes=32 << 20),
        cost_estimate=pl.CostEstimate(flops=1_100_000_000, bytes_accessed=2_100_000, transcendentals=0),
        name="permute",
    )(x, source.reshape(-1, 1))


def regroup_kernel(x_ref, out_ref, places_ref, joined):
    pieces = x_ref.shape[0]
    rows, width = joined.shape
    body = SIDE * width // LANES
    for i in range(pieces):
        for c in range(width // LANES):
            joined[i * SIDE : (i + 1) * SIDE, c * LANES : (c + 1) * LANES] = x_ref[i, c * SIDE : (c + 1) * SIDE, :]
    high, low = [], []
    for i in range(0, pieces, LANES // SIDE):
        notes = [x_ref[i + k, body:, :].astype(jnp.float32) for k in range(LANES // SIDE)]
        note = functools.reduce(jnp.add, notes)
        high.append(note[0:1, :])
        low.append(note[1:2, :])
    places = (jnp.concatenate(high, axis=1) * 32.0 + jnp.concatenate(low, axis=1)).astype(jnp.int32)
    places_ref[...] = jnp.broadcast_to(places, places_ref.shape)
    for tile in range(rows // TILE):
        own = lax.broadcasted_iota(jnp.int32, (TILE, rows), 0) + tile * TILE
        chosen = jnp.where(own == places, 1.0, 0.0).astype(jnp.bfloat16)
        out_ref[tile * TILE : (tile + 1) * TILE, :] = jnp.dot(
            chosen, joined[...], preferred_element_type=jnp.float32
        ).astype(jnp.bfloat16)


def regroup_rows(x, rows, width):
    vmem = pl.BlockSpec(memory_space=pltpu.VMEM)
    return pl.pallas_call(
        regroup_kernel,
        out_shape=(jax.ShapeDtypeStruct((rows, width), x.dtype), jax.ShapeDtypeStruct((8, rows), jnp.int32)),
        in_specs=[vmem],
        out_specs=(vmem, vmem),
        scratch_shapes=[pltpu.VMEM((rows, width), jnp.bfloat16)],
        compiler_params=pltpu.CompilerParams(vmem_limit_bytes=32 << 20),
        cost_estimate=pl.CostEstimate(flops=1_100_000_000, bytes_accessed=2_200_000, transcendentals=0),
        name="regroup",
    )(x)


def pick_kernel(source_ref, x_ref, out_ref, sems):
    copies = [
        pltpu.make_async_copy(x_ref.at[source_ref[q]], out_ref.at[q], sems.at[q]) for q in range(out_ref.shape[0])
    ]
    for copy in copies:
        copy.start()
    for copy in copies:
        copy.wait()


def pick_parts(x, source):
    count = source.shape[0]
    return pl.pallas_call(
        pick_kernel,
        out_shape=jax.ShapeDtypeStruct((count,) + x.shape[1:], x.dtype),
        in_specs=[pl.BlockSpec(memory_space=pltpu.SMEM), pl.BlockSpec(memory_space=pl.ANY)],
        out_specs=pl.BlockSpec(memory_space=pltpu.VMEM),
        scratch_shapes=[pltpu.SemaphoreType.DMA((count,))],
        compiler_params=pltpu.CompilerParams(vmem_limit_bytes=32 << 20),
        cost_estimate=pl.CostEstimate(flops=0, bytes_accessed=2_100_000, transcendentals=0),
        name="pick",
    )(source, x)


def homeward_kernel(owner_ref, live_ref, x_ref, out_ref):
    groups, slots, part, width = out_ref.shape
    quarter = part // SIDE
    row = lax.broadcasted_iota(jnp.int32, (part, part), 0)
    column = lax.broadcasted_iota(jnp.int32, (part, part), 1)
    order = jnp.where(column == (row % SIDE) * quarter + row // SIDE, 1.0, 0.0).astype(jnp.bfloat16)
    for g in range(groups):
        for s in range(slots):
            start = pl.multiple_of(owner_ref[g * slots + s] * part, part)
            piece = jnp.dot(order, x_ref[pl.ds(start, part), :], preferred_element_type=jnp.float32)
            keep = live_ref[g * slots + s] > 0
            out_ref[g, s] = jnp.where(keep, piece, 0.0).astype(jnp.bfloat16)


def homeward_parts(x, owner, live, groups, slots):
    rows, width = x.shape
    smem = pl.BlockSpec(memory_space=pltpu.SMEM)
    vmem = pl.BlockSpec(memory_space=pltpu.VMEM)
    return pl.pallas_call(
        homeward_kernel,
        out_shape=jax.ShapeDtypeStruct((groups, slots, rows // groups, width), x.dtype),
        in_specs=[smem, smem, vmem],
        out_specs=vmem,
        compiler_params=pltpu.CompilerParams(vmem_limit_bytes=32 << 20),
        cost_estimate=pl.CostEstimate(flops=270_000_000, bytes_accessed=3_200_000, transcendentals=0),
        name="homeward",
    )(owner, live, x)


def exchange(x, axis):
    return lax.all_to_all(x, axis, split_axis=0, concat_axis=0, tiled=True)


def body(
    home_points,
    counts,
    owner_group,
    neighbors_home,
    hilbert_target,
    neighbors_second,
    depth_first,
    mixing_first,
    gain_first,
    w_qkv_first,
    w_out_first,
    depth_second,
    mixing_second,
    gain_second,
    w_qkv_second,
    w_out_second,
):
    groups = lax.axis_size("grp")
    owners = lax.axis_size("dev")
    home_rows, width = home_points.shape
    slots = owner_group.shape[0]
    rows = home_rows // slots
    blocks = hilbert_target.shape[0]
    part = rows // groups
    side = rows // owners
    first_params = (depth_first, mixing_first, gain_first, w_qkv_first, w_out_first)
    second_params = (depth_second, mixing_second, gain_second, w_qkv_second, w_out_second)

    letters = enclosed(neighbors_home, jnp.concatenate([counts, owner_group]), slots, groups, width)
    points = jnp.concatenate([home_points.reshape(slots, groups, part, width), letters], axis=2)
    spread = exchange(jnp.transpose(points, (1, 0, 2, 3)), "grp")
    plan = spread[:, 0, part + LIST_ROWS, : 1 + slots].astype(jnp.int32)
    live = (jnp.arange(slots)[None, :] < plan[:, :1]).reshape(-1)
    owner = plan[:, 1:].reshape(-1)
    match = live[None, :] & (owner[None, :] == jnp.arange(groups)[:, None])
    source = jnp.sum(jnp.where(match, jnp.arange(groups * slots)[None, :], 0), axis=1)
    owned = exchange(pick_parts(spread.reshape((groups * slots,) + spread.shape[2:]), source), "grp")

    arrival = (neighbors_second % side) * side + neighbors_second // side
    second_lists = staged(arrival, rows)
    column = lax.axis_index("dev")
    pair = jnp.arange(2)[None, :]
    places = (2 * hilbert_target[:, None] + pair).reshape(1, -1)
    digits = jnp.concatenate([places // 32, places % 32, jnp.zeros((NOTE_ROWS - 2, side), jnp.int32)])
    mine = jnp.arange(LANES // side) == column % (LANES // side)
    note = jnp.where(mine[None, :, None], digits[:, None, :], 0).reshape(NOTE_ROWS, LANES).astype(jnp.bfloat16)

    section_one = encoder_block(owned, note, first_params, rows, True)
    mid, places = regroup_rows(exchange(section_one, "dev"), rows, width)
    targets = places[0].reshape(owners, blocks, 2)[:, :, 0] // 2
    by_part = jnp.transpose(targets.reshape(owners, groups, -1), (1, 0, 2)).reshape(-1, 1)
    backward_rows = (2 * by_part + pair).reshape(-1)
    regrouped = exchange(mid.reshape(owners, side, width), "dev").reshape(rows, width)
    section_two = encoder_block(regrouped, second_lists, second_params, rows, False)
    mid = exchange(section_two.reshape(owners, side, width), "dev").reshape(rows, width)
    mid = permute_rows(mid, backward_rows)
    returned = exchange(mid.reshape(groups * owners, -1, width), ("grp", "dev")).reshape(rows, width)
    homeward = homeward_parts(returned, owner, live.astype(jnp.int32), groups, slots)
    delivered = exchange(homeward, "grp")
    return jnp.transpose(delivered, (1, 0, 2, 3)).reshape(home_rows, width)


def solution(mesh):
    return jax.shard_map(
        body,
        mesh=mesh,
        in_specs=(
            P(("grp", "dev"), None),
            P(("grp", "dev")),
            P(("grp", "dev")),
            P(None, ("grp", "dev")),
            P(("grp", "dev")),
            P(None, ("grp", "dev")),
            P(),
            P(),
            P(),
            P(),
            P(),
            P(),
            P(),
            P(),
            P(),
            P(),
        ),
        out_specs=P(("grp", "dev"), None),
        check_vma=False,
    )
```

```python
import functools
import jax
import jax.numpy as jnp
from jax import lax
from jax.experimental import pallas as pl
from jax.experimental.pallas import tpu as pltpu
from jax.sharding import PartitionSpec as P

HEADS = 8
HEAD_DIM = 64
epsilon = 1e-05
SCALE = HEAD_DIM ** (-0.5) * 1.4426950408889634
LANES = 128
TILE = 512
SIDE = 32
CHUNK = 128
BUFFERS = 2
LIST_ROWS = 14
NOTE_ROWS = 8


def block_kernel(first, *refs):
    if first:
        (
            x_ref, note_ref, depth_ref, mixing_ref, gain_ref, w_qkv_ref, w_out_ref, out_ref,
            plain, summed, updated, project, mixed, scores_even, scores_odd, powers_even, powers_odd, lists_ref, *stage
        ) = refs
    else:
        (
            lists_ref, x_ref, depth_ref, mixing_ref, gain_ref, w_qkv_ref, w_out_ref, out_ref,
            plain, summed, updated, project, mixed, scores_even, scores_odd, powers_even, powers_odd, *stage
        ) = refs
    buffers, sems = stage[:BUFFERS], stage[BUFFERS]
    rows, width = updated.shape
    fanout = depth_ref.shape[0]
    chunks = width // LANES
    pairs = width // LANES
    tiles = rows // TILE
    count = rows // CHUNK
    if first:
        parts = x_ref.shape[0]
        part = rows // parts
        halves = parts // 4

        def digits(block):
            upper = x_ref[2 * block, part : part + LIST_ROWS, :]
            lower = x_ref[2 * block + 1, part : part + LIST_ROWS, :]
            return upper.astype(jnp.float32), lower.astype(jnp.float32)

        for half in range(halves):
            high, low = digits(half), digits(halves + half)
            for piece in range(2):
                found = ((high[piece] * 32.0 + low[piece]) * chunks).astype(jnp.int32)
                kept = min(LIST_ROWS, fanout - piece * LIST_ROWS)
                for c in range(chunks):
                    lists_ref[half * chunks + c, piece * LIST_ROWS : piece * LIST_ROWS + kept, :] = found[
                        :kept, c * LANES : (c + 1) * LANES
                    ]

    def fetch(chunk, slot):
        return pltpu.make_async_copy(lists_ref.at[chunk], buffers[slot], sems.at[slot])

    for slot in range(BUFFERS):
        fetch(slot, slot).start()
    for c in range(chunks):
        cols = slice(c * LANES, (c + 1) * LANES)
        if first:
            for p in range(parts):
                plain[pl.ds(p * part * chunks + c, part, stride=chunks), :] = x_ref[p, :part, cols].astype(jnp.float32)
        else:
            plain[pl.ds(c, rows, stride=chunks), :] = x_ref[:, cols].astype(jnp.float32)

    def gather(step, carry):
        for slot in range(BUFFERS):
            chunk = step * BUFFERS + slot
            fetch(chunk, slot).wait()
            base = pl.multiple_of(chunk * (CHUNK // SIDE) * chunks, (CHUNK // SIDE) * chunks)
            for u in range(CHUNK):
                total = None
                for j in range(fanout):
                    term = plain[pl.ds(buffers[slot][j, u], chunks), :] * depth_ref[j]
                    total = term if total is None else total + term
                summed[pl.ds(base + ((u % SIDE) * SIDE + u // SIDE) * chunks, chunks), :] = total

            @pl.when(chunk + BUFFERS < count)
            def _():
                fetch(chunk + BUFFERS, slot).start()

        return carry

    lax.fori_loop(0, count // BUFFERS, gather, 0)

    def head(tile, carry):
        row0 = pl.multiple_of(tile * TILE, TILE)
        encoded = jnp.concatenate(
            [summed[pl.ds(row0 * chunks + c, TILE, stride=chunks), :] for c in range(chunks)], axis=1
        ).astype(jnp.bfloat16)
        if first:
            groups = TILE // SIDE
            residual = jnp.concatenate(
                [
                    jnp.concatenate(
                        [
                            plain[pl.ds((tile * groups + g) * chunks + c, SIDE, stride=SIDE * chunks), :]
                            for g in range(groups)
                        ],
                        axis=0,
                    )
                    for c in range(chunks)
                ],
                axis=1,
            )
        else:
            residual = x_ref[pl.ds(row0, TILE), :].astype(jnp.float32)
        up = residual + jnp.dot(encoded, mixing_ref[...], preferred_element_type=jnp.float32)
        updated[pl.ds(row0, TILE), :] = up
        centre = jnp.mean(up, axis=-1, keepdims=True)
        off = up - centre
        spread = jnp.mean(off * off, axis=-1, keepdims=True)
        normed = (off * lax.rsqrt(spread + epsilon) * gain_ref[...]).astype(jnp.bfloat16)
        project[pl.ds(row0, TILE), :width] = (
            jnp.dot(normed, w_qkv_ref[:, :width], preferred_element_type=jnp.float32) * SCALE
        ).astype(jnp.bfloat16)
        project[pl.ds(row0, TILE), width:] = jnp.dot(
            normed, w_qkv_ref[:, width:], preferred_element_type=jnp.float32
        ).astype(jnp.bfloat16)
        return carry

    lax.fori_loop(0, tiles, head, 0)
    left = lax.broadcasted_iota(jnp.int32, (TILE, LANES), 1) < HEAD_DIM
    ones = jnp.ones((rows, LANES), jnp.bfloat16)

    def place(step):
        row0 = pl.multiple_of(lax.rem(step, tiles) * TILE, TILE)
        col0 = pl.multiple_of(lax.div(step, tiles) * LANES, LANES)
        return row0, col0

    def score(step, half, target):
        row0, col0 = place(step)
        queries = project[pl.ds(row0, TILE), pl.ds(col0, LANES)]
        keep = left if half == 0 else jnp.logical_not(left)
        own = jnp.where(keep, queries, jnp.zeros((), jnp.bfloat16))
        keys = project[:, pl.ds(width + col0, LANES)]
        target[...] = lax.dot_general(own, keys, (((1,), (1,)), ((), ())), preferred_element_type=jnp.float32)

    def weigh(source, target):
        scores = source[...]
        peak = jnp.max(scores, axis=-1, keepdims=True)
        target[...] = jnp.exp2(scores - peak).astype(jnp.bfloat16)

    def blend(step, half, source):
        row0, col0 = place(step)
        values = jnp.concatenate([project[:, pl.ds(2 * width + col0, LANES)], ones], axis=1)
        both = jnp.dot(source[...], values, preferred_element_type=jnp.float32)
        result = (both[:, :LANES] / both[:, LANES:]).astype(jnp.bfloat16)
        keep = left if half == 0 else jnp.logical_not(left)
        spot = (pl.ds(row0, TILE), pl.ds(col0, LANES))
        mixed[spot] = jnp.where(keep, result, mixed[spot])

    last = pairs * tiles - 1
    score(0, 0, scores_even)
    powers_odd[...] = jnp.ones_like(powers_odd)

    def attend(step, carry):
        score(step, 1, scores_odd)
        weigh(scores_even, powers_even)
        blend(jnp.maximum(step - 1, 0), 1, powers_odd)
        score(jnp.minimum(step + 1, last), 0, scores_even)
        weigh(scores_odd, powers_odd)
        blend(step, 0, powers_even)
        return carry

    lax.fori_loop(0, pairs * tiles, attend, 0)
    blend(last, 1, powers_odd)

    def tail(tile, carry):
        row0 = pl.multiple_of(tile * TILE, TILE)
        result = (
            updated[pl.ds(row0, TILE), :]
            + jnp.dot(mixed[pl.ds(row0, TILE), :], w_out_ref[...], preferred_element_type=jnp.float32)
        ).astype(jnp.bfloat16)
        if first:
            for i in range(TILE // SIDE):
                for c in range(chunks):
                    out_ref[tile * (TILE // SIDE) + i, c * SIDE : (c + 1) * SIDE, :] = result[
                        i * SIDE : (i + 1) * SIDE, c * LANES : (c + 1) * LANES
                    ]
        else:
            out_ref[pl.ds(row0, TILE), :] = result
        return carry

    lax.fori_loop(0, tiles, tail, 0)
    if first:
        for i in range(rows // SIDE):
            out_ref[i, chunks * SIDE :, :] = note_ref[...]


def encoder_block(features, beside, params, rows, first):
    depth, mixing, gain, w_qkv, w_out = params
    fanout, width = depth.shape
    vmem = pl.BlockSpec(memory_space=pltpu.VMEM)
    table = (rows // CHUNK, SIDE, LANES)
    operands = (depth.reshape(fanout, -1, LANES), mixing, gain.reshape(1, width), w_qkv, w_out)
    operands = ((features, beside) if first else (beside, features)) + operands
    shape = (rows // SIDE, SIDE * width // LANES + NOTE_ROWS, LANES) if first else (rows, width)
    return pl.pallas_call(
        functools.partial(block_kernel, first),
        out_shape=jax.ShapeDtypeStruct(shape, jnp.bfloat16),
        in_specs=[vmem] * len(operands),
        out_specs=vmem,
        scratch_shapes=[
            pltpu.VMEM((rows * 4, LANES), jnp.float32),
            pltpu.VMEM((rows * 4, LANES), jnp.float32),
            pltpu.VMEM((rows, width), jnp.float32),
            pltpu.VMEM((rows, 3 * width), jnp.bfloat16),
            pltpu.VMEM((rows, width), jnp.bfloat16),
            pltpu.VMEM((TILE, rows), jnp.float32),
            pltpu.VMEM((TILE, rows), jnp.float32),
            pltpu.VMEM((TILE, rows), jnp.bfloat16),
            pltpu.VMEM((TILE, rows), jnp.bfloat16),
        ]
        + [pltpu.VMEM(table, jnp.int32)] * first
        + [pltpu.SMEM(table[1:], jnp.int32)] * BUFFERS
        + [pltpu.SemaphoreType.DMA((BUFFERS,))],
        compiler_params=pltpu.CompilerParams(vmem_limit_bytes=30 << 20),
        cost_estimate=pl.CostEstimate(flops=5_000_000_000, bytes_accessed=6_000_000, transcendentals=8_000_000),
        name="block",
    )(*operands)


def staged(lists, rows):
    fanout = lists.shape[0]
    table = jnp.transpose((lists * 4).reshape(fanout, rows // CHUNK, LANES), (1, 0, 2))
    return jnp.pad(table, ((0, 0), (0, SIDE - fanout), (0, 0)))


def enclosed(neighbors, plan, slots, groups, width):
    fanout = neighbors.shape[0]
    lists = jnp.transpose(neighbors.reshape(fanout, slots, -1, width), (1, 2, 0, 3))
    lists = jnp.pad(lists, ((0, 0), (0, 0), (0, 2 * LIST_ROWS - fanout), (0, 0)))
    letters = jnp.concatenate([lists // 32, lists % 32], axis=1).reshape(slots, groups, LIST_ROWS, width)
    note = jnp.broadcast_to(jnp.pad(plan, (0, width - plan.shape[0])), (slots, groups, 2, width))
    return jnp.concatenate([letters, note], axis=2).astype(jnp.bfloat16)


def permute_kernel(x_ref, source_ref, out_ref):
    rows = x_ref.shape[0]
    positions = lax.broadcasted_iota(jnp.int32, (TILE, rows), 1)
    for tile in range(rows // TILE):
        own = slice(tile * TILE, (tile + 1) * TILE)
        chosen = jnp.where(positions == source_ref[own, :], 1.0, 0.0).astype(jnp.bfloat16)
        out_ref[own, :] = jnp.dot(chosen, x_ref[...], preferred_element_type=jnp.float32).astype(jnp.bfloat16)


def permute_rows(x, source):
    vmem = pl.BlockSpec(memory_space=pltpu.VMEM)
    return pl.pallas_call(
        permute_kernel,
        out_shape=jax.ShapeDtypeStruct(x.shape, x.dtype),
        in_specs=[vmem, vmem],
        out_specs=vmem,
        compiler_params=pltpu.CompilerParams(vmem_limit_bytes=16 << 20),
        cost_estimate=pl.CostEstimate(flops=1_100_000_000, bytes_accessed=2_100_000, transcendentals=0),
        name="permute",
    )(x, source.reshape(-1, 1))


def regroup_kernel(x_ref, out_ref, places_ref, joined):
    pieces = x_ref.shape[0]
    rows, width = joined.shape
    body = SIDE * width // LANES
    for i in range(pieces):
        for c in range(width // LANES):
            joined[i * SIDE : (i + 1) * SIDE, c * LANES : (c + 1) * LANES] = x_ref[i, c * SIDE : (c + 1) * SIDE, :]
    high, low = [], []
    for i in range(0, pieces, LANES // SIDE):
        notes = [x_ref[i + k, body:, :].astype(jnp.float32) for k in range(LANES // SIDE)]
        note = functools.reduce(jnp.add, notes)
        high.append(note[0:1, :])
        low.append(note[1:2, :])
    places = (jnp.concatenate(high, axis=1) * 32.0 + jnp.concatenate(low, axis=1)).astype(jnp.int32)
    places_ref[...] = jnp.broadcast_to(places, places_ref.shape)
    for tile in range(rows // TILE):
        own = lax.broadcasted_iota(jnp.int32, (TILE, rows), 0) + tile * TILE
        chosen = jnp.where(own == places, 1.0, 0.0).astype(jnp.bfloat16)
        out_ref[tile * TILE : (tile + 1) * TILE, :] = jnp.dot(
            chosen, joined[...], preferred_element_type=jnp.float32
        ).astype(jnp.bfloat16)


def regroup_rows(x, rows, width):
    vmem = pl.BlockSpec(memory_space=pltpu.VMEM)
    return pl.pallas_call(
        regroup_kernel,
        out_shape=(jax.ShapeDtypeStruct((rows, width), x.dtype), jax.ShapeDtypeStruct((8, rows), jnp.int32)),
        in_specs=[vmem],
        out_specs=(vmem, vmem),
        scratch_shapes=[pltpu.VMEM((rows, width), jnp.bfloat16)],
        compiler_params=pltpu.CompilerParams(vmem_limit_bytes=16 << 20),
        cost_estimate=pl.CostEstimate(flops=1_100_000_000, bytes_accessed=2_200_000, transcendentals=0),
        name="regroup",
    )(x)


def pick_kernel(source_ref, x_ref, out_ref):
    for q in range(out_ref.shape[0]):
        out_ref[q] = x_ref[source_ref[q]]


def pick_parts(x, source):
    vmem = pl.BlockSpec(memory_space=pltpu.VMEM)
    return pl.pallas_call(
        pick_kernel,
        out_shape=jax.ShapeDtypeStruct((source.shape[0],) + x.shape[1:], x.dtype),
        in_specs=[pl.BlockSpec(memory_space=pltpu.SMEM), vmem],
        out_specs=vmem,
        compiler_params=pltpu.CompilerParams(vmem_limit_bytes=16 << 20),
        cost_estimate=pl.CostEstimate(flops=0, bytes_accessed=2_300_000, transcendentals=0),
        name="pick",
    )(source, x)


def homeward_kernel(owner_ref, live_ref, x_ref, out_ref):
    groups, slots, part, width = out_ref.shape
    quarter = part // SIDE
    row = lax.broadcasted_iota(jnp.int32, (part, part), 0)
    column = lax.broadcasted_iota(jnp.int32, (part, part), 1)
    order = jnp.where(column == (row % SIDE) * quarter + row // SIDE, 1.0, 0.0).astype(jnp.bfloat16)
    for g in range(groups):
        for s in range(slots):
            start = pl.multiple_of(owner_ref[g * slots + s] * part, part)
            piece = jnp.dot(order, x_ref[pl.ds(start, part), :], preferred_element_type=jnp.float32)
            keep = live_ref[g * slots + s] > 0
            out_ref[g, s] = jnp.where(keep, piece, 0.0).astype(jnp.bfloat16)


def homeward_parts(x, owner, live, groups, slots):
    rows, width = x.shape
    smem = pl.BlockSpec(memory_space=pltpu.SMEM)
    vmem = pl.BlockSpec(memory_space=pltpu.VMEM)
    return pl.pallas_call(
        homeward_kernel,
        out_shape=jax.ShapeDtypeStruct((groups, slots, rows // groups, width), x.dtype),
        in_specs=[smem, smem, vmem],
        out_specs=vmem,
        compiler_params=pltpu.CompilerParams(vmem_limit_bytes=16 << 20),
        cost_estimate=pl.CostEstimate(flops=270_000_000, bytes_accessed=3_200_000, transcendentals=0),
        name="homeward",
    )(owner, live, x)


def exchange(x, axis):
    return lax.all_to_all(x, axis, split_axis=0, concat_axis=0, tiled=True)


def body(
    home_points,
    counts,
    owner_group,
    neighbors_home,
    hilbert_target,
    neighbors_second,
    depth_first,
    mixing_first,
    gain_first,
    w_qkv_first,
    w_out_first,
    depth_second,
    mixing_second,
    gain_second,
    w_qkv_second,
    w_out_second,
):
    groups = lax.axis_size("grp")
    owners = lax.axis_size("dev")
    home_rows, width = home_points.shape
    slots = owner_group.shape[0]
    rows = home_rows // slots
    blocks = hilbert_target.shape[0]
    part = rows // groups
    side = rows // owners
    first_params = (depth_first, mixing_first, gain_first, w_qkv_first, w_out_first)
    second_params = (depth_second, mixing_second, gain_second, w_qkv_second, w_out_second)

    letters = enclosed(neighbors_home, jnp.concatenate([counts, owner_group]), slots, groups, width)
    points = jnp.concatenate([home_points.reshape(slots, groups, part, width), letters], axis=2)
    spread = exchange(jnp.transpose(points, (1, 0, 2, 3)), "grp")
    plan = spread[:, 0, part + LIST_ROWS, : 1 + slots].astype(jnp.int32)
    live = (jnp.arange(slots)[None, :] < plan[:, :1]).reshape(-1)
    owner = plan[:, 1:].reshape(-1)
    match = live[None, :] & (owner[None, :] == jnp.arange(groups)[:, None])
    source = jnp.sum(jnp.where(match, jnp.arange(groups * slots)[None, :], 0), axis=1)
    owned = exchange(pick_parts(spread.reshape((groups * slots,) + spread.shape[2:]), source), "grp")

    arrival = (neighbors_second % side) * side + neighbors_second // side
    second_lists = staged(arrival, rows)
    column = lax.axis_index("dev")
    pair = jnp.arange(2)[None, :]
    places = (2 * hilbert_target[:, None] + pair).reshape(1, -1)
    digits = jnp.concatenate([places // 32, places % 32, jnp.zeros((NOTE_ROWS - 2, side), jnp.int32)])
    mine = jnp.arange(LANES // side) == column % (LANES // side)
    note = jnp.where(mine[None, :, None], digits[:, None, :], 0).reshape(NOTE_ROWS, LANES).astype(jnp.bfloat16)

    section_one = encoder_block(owned, note, first_params, rows, True)
    mid, places = regroup_rows(exchange(section_one, "dev"), rows, width)
    targets = places[0].reshape(owners, blocks, 2)[:, :, 0] // 2
    by_part = jnp.transpose(targets.reshape(owners, groups, -1), (1, 0, 2)).reshape(-1, 1)
    backward_rows = (2 * by_part + pair).reshape(-1)
    regrouped = exchange(mid.reshape(owners, side, width), "dev").reshape(rows, width)
    section_two = encoder_block(regrouped, second_lists, second_params, rows, False)
    mid = exchange(section_two.reshape(owners, side, width), "dev").reshape(rows, width)
    mid = permute_rows(mid, backward_rows)
    returned = exchange(mid.reshape(groups * owners, -1, width), ("grp", "dev")).reshape(rows, width)
    homeward = homeward_parts(returned, owner, live.astype(jnp.int32), groups, slots)
    delivered = exchange(homeward, "grp")
    return jnp.transpose(delivered, (1, 0, 2, 3)).reshape(home_rows, width)


def solution(mesh):
    return jax.shard_map(
        body,
        mesh=mesh,
        in_specs=(
            P(("grp", "dev"), None),
            P(("grp", "dev")),
            P(("grp", "dev")),
            P(None, ("grp", "dev")),
            P(("grp", "dev")),
            P(None, ("grp", "dev")),
            P(),
            P(),
            P(),
            P(),
            P(),
            P(),
            P(),
            P(),
            P(),
            P(),
        ),
        out_specs=P(("grp", "dev"), None),
        check_vma=False,
    )
```

```python
import functools
import jax
import jax.numpy as jnp
from jax import lax
from jax.experimental import pallas as pl
from jax.experimental.pallas import tpu as pltpu
from jax.sharding import PartitionSpec as P

HEADS = 8
HEAD_DIM = 64
epsilon = 1e-05
SCALE = HEAD_DIM ** (-0.5) * 1.4426950408889634
LANES = 128
TILE = 512
SIDE = 32
CHUNK = 128
BUFFERS = 2
LIST_ROWS = 14
NOTE_ROWS = 8


def block_kernel(first, *refs):
    if first:
        (
            x_ref, note_ref, depth_ref, mixing_ref, gain_ref, w_q_ref, w_k_ref, w_v_ref, w_out_ref, out_ref,
            plain, summed, updated, project, mixed, scores_even, scores_odd, powers_even, powers_odd, lists_ref, *stage
        ) = refs
    else:
        (
            lists_ref, x_ref, depth_ref, mixing_ref, gain_ref, w_q_ref, w_k_ref, w_v_ref, w_out_ref, out_ref,
            plain, summed, updated, project, mixed, scores_even, scores_odd, powers_even, powers_odd, *stage
        ) = refs
    buffers, sems = stage[:BUFFERS], stage[BUFFERS]
    rows, width = updated.shape
    fanout = depth_ref.shape[0]
    chunks = width // LANES
    pairs = width // LANES
    tiles = rows // TILE
    count = rows // CHUNK
    if first:
        parts = x_ref.shape[0]
        part = rows // parts
        halves = parts // 4

        def digits(block):
            upper = x_ref[2 * block, part : part + LIST_ROWS, :]
            lower = x_ref[2 * block + 1, part : part + LIST_ROWS, :]
            return upper.astype(jnp.float32), lower.astype(jnp.float32)

        for half in range(halves):
            high, low = digits(half), digits(halves + half)
            for piece in range(2):
                found = ((high[piece] * 32.0 + low[piece]) * chunks).astype(jnp.int32)
                kept = min(LIST_ROWS, fanout - piece * LIST_ROWS)
                for c in range(chunks):
                    lists_ref[half * chunks + c, piece * LIST_ROWS : piece * LIST_ROWS + kept, :] = found[
                        :kept, c * LANES : (c + 1) * LANES
                    ]

    def fetch(chunk, slot):
        return pltpu.make_async_copy(lists_ref.at[chunk], buffers[slot], sems.at[slot])

    for slot in range(BUFFERS):
        fetch(slot, slot).start()
    for c in range(chunks):
        cols = slice(c * LANES, (c + 1) * LANES)
        if first:
            for p in range(parts):
                plain[pl.ds(p * part * chunks + c, part, stride=chunks), :] = x_ref[p, :part, cols].astype(jnp.float32)
        else:
            plain[pl.ds(c, rows, stride=chunks), :] = x_ref[:, cols].astype(jnp.float32)

    def gather(step, carry):
        for slot in range(BUFFERS):
            chunk = step * BUFFERS + slot
            fetch(chunk, slot).wait()
            base = pl.multiple_of(chunk * (CHUNK // SIDE) * chunks, (CHUNK // SIDE) * chunks)
            for u in range(CHUNK):
                total = None
                for j in range(fanout):
                    term = plain[pl.ds(buffers[slot][j, u], chunks), :] * depth_ref[j]
                    total = term if total is None else total + term
                summed[pl.ds(base + ((u % SIDE) * SIDE + u // SIDE) * chunks, chunks), :] = total

            @pl.when(chunk + BUFFERS < count)
            def _():
                fetch(chunk + BUFFERS, slot).start()

        return carry

    lax.fori_loop(0, count // BUFFERS, gather, 0)

    def head(tile, carry):
        row0 = pl.multiple_of(tile * TILE, TILE)
        encoded = jnp.concatenate(
            [summed[pl.ds(row0 * chunks + c, TILE, stride=chunks), :] for c in range(chunks)], axis=1
        ).astype(jnp.bfloat16)
        if first:
            groups = TILE // SIDE
            residual = jnp.concatenate(
                [
                    jnp.concatenate(
                        [
                            plain[pl.ds((tile * groups + g) * chunks + c, SIDE, stride=SIDE * chunks), :]
                            for g in range(groups)
                        ],
                        axis=0,
                    )
                    for c in range(chunks)
                ],
                axis=1,
            )
        else:
            residual = x_ref[pl.ds(row0, TILE), :].astype(jnp.float32)
        up = residual + jnp.dot(encoded, mixing_ref[...], preferred_element_type=jnp.float32)
        updated[pl.ds(row0, TILE), :] = up
        centre = jnp.mean(up, axis=-1, keepdims=True)
        off = up - centre
        spread = jnp.mean(off * off, axis=-1, keepdims=True)
        normed = (off * lax.rsqrt(spread + epsilon) * gain_ref[...]).astype(jnp.bfloat16)
        project[pl.ds(row0, TILE), :width] = (
            jnp.dot(normed, w_q_ref[...], preferred_element_type=jnp.float32) * SCALE
        ).astype(jnp.bfloat16)
        for side, w_ref in ((1, w_k_ref), (2, w_v_ref)):
            project[pl.ds(row0, TILE), side * width : (side + 1) * width] = jnp.dot(
                normed, w_ref[...], preferred_element_type=jnp.float32
            ).astype(jnp.bfloat16)
        return carry

    lax.fori_loop(0, tiles, head, 0)
    left = lax.broadcasted_iota(jnp.int32, (TILE, LANES), 1) < HEAD_DIM
    ones = jnp.ones((rows, LANES), jnp.bfloat16)

    def place(step):
        row0 = pl.multiple_of(lax.rem(step, tiles) * TILE, TILE)
        col0 = pl.multiple_of(lax.div(step, tiles) * LANES, LANES)
        return row0, col0

    def score(step, half, target):
        row0, col0 = place(step)
        queries = project[pl.ds(row0, TILE), pl.ds(col0, LANES)]
        keep = left if half == 0 else jnp.logical_not(left)
        own = jnp.where(keep, queries, jnp.zeros((), jnp.bfloat16))
        keys = project[:, pl.ds(width + col0, LANES)]
        target[...] = lax.dot_general(own, keys, (((1,), (1,)), ((), ())), preferred_element_type=jnp.float32)

    def weigh(source, target):
        scores = source[...]
        peak = jnp.max(scores, axis=-1, keepdims=True)
        target[...] = jnp.exp2(scores - peak).astype(jnp.bfloat16)

    def blend(step, half, source):
        row0, col0 = place(step)
        values = jnp.concatenate([project[:, pl.ds(2 * width + col0, LANES)], ones], axis=1)
        both = jnp.dot(source[...], values, preferred_element_type=jnp.float32)
        result = (both[:, :LANES] / both[:, LANES:]).astype(jnp.bfloat16)
        keep = left if half == 0 else jnp.logical_not(left)
        spot = (pl.ds(row0, TILE), pl.ds(col0, LANES))
        mixed[spot] = jnp.where(keep, result, mixed[spot])

    last = pairs * tiles - 1
    score(0, 0, scores_even)
    powers_odd[...] = jnp.ones_like(powers_odd)

    def attend(step, carry):
        score(step, 1, scores_odd)
        weigh(scores_even, powers_even)
        blend(jnp.maximum(step - 1, 0), 1, powers_odd)
        score(jnp.minimum(step + 1, last), 0, scores_even)
        weigh(scores_odd, powers_odd)
        blend(step, 0, powers_even)
        return carry

    lax.fori_loop(0, pairs * tiles, attend, 0)
    blend(last, 1, powers_odd)

    def tail(tile, carry):
        row0 = pl.multiple_of(tile * TILE, TILE)
        result = (
            updated[pl.ds(row0, TILE), :]
            + jnp.dot(mixed[pl.ds(row0, TILE), :], w_out_ref[...], preferred_element_type=jnp.float32)
        ).astype(jnp.bfloat16)
        if first:
            for i in range(TILE // SIDE):
                for c in range(chunks):
                    out_ref[tile * (TILE // SIDE) + i, c * SIDE : (c + 1) * SIDE, :] = result[
                        i * SIDE : (i + 1) * SIDE, c * LANES : (c + 1) * LANES
                    ]
        else:
            out_ref[pl.ds(row0, TILE), :] = result
        return carry

    lax.fori_loop(0, tiles, tail, 0)
    if first:
        for i in range(rows // SIDE):
            out_ref[i, chunks * SIDE :, :] = note_ref[...]


def encoder_block(features, beside, params, rows, first):
    depth, mixing, gain, w_qkv, w_out = params
    fanout, width = depth.shape
    vmem = pl.BlockSpec(memory_space=pltpu.VMEM)
    table = (rows // CHUNK, SIDE, LANES)
    operands = (depth.reshape(fanout, -1, LANES), mixing, gain.reshape(1, width), *jnp.split(w_qkv, 3, axis=1), w_out)
    operands = ((features, beside) if first else (beside, features)) + operands
    shape = (rows // SIDE, SIDE * width // LANES + NOTE_ROWS, LANES) if first else (rows, width)
    return pl.pallas_call(
        functools.partial(block_kernel, first),
        out_shape=jax.ShapeDtypeStruct(shape, jnp.bfloat16),
        in_specs=[vmem] * len(operands),
        out_specs=vmem,
        scratch_shapes=[
            pltpu.VMEM((rows * 4, LANES), jnp.float32),
            pltpu.VMEM((rows * 4, LANES), jnp.float32),
            pltpu.VMEM((rows, width), jnp.float32),
            pltpu.VMEM((rows, 3 * width), jnp.bfloat16),
            pltpu.VMEM((rows, width), jnp.bfloat16),
            pltpu.VMEM((TILE, rows), jnp.float32),
            pltpu.VMEM((TILE, rows), jnp.float32),
            pltpu.VMEM((TILE, rows), jnp.bfloat16),
            pltpu.VMEM((TILE, rows), jnp.bfloat16),
        ]
        + [pltpu.VMEM(table, jnp.int32)] * first
        + [pltpu.SMEM(table[1:], jnp.int32)] * BUFFERS
        + [pltpu.SemaphoreType.DMA((BUFFERS,))],
        compiler_params=pltpu.CompilerParams(vmem_limit_bytes=30 << 20),
        cost_estimate=pl.CostEstimate(flops=5_000_000_000, bytes_accessed=6_000_000, transcendentals=8_000_000),
        name="block",
    )(*operands)


def staged(lists, rows):
    fanout = lists.shape[0]
    table = jnp.transpose((lists * 4).reshape(fanout, rows // CHUNK, LANES), (1, 0, 2))
    return jnp.pad(table, ((0, 0), (0, SIDE - fanout), (0, 0)))


def enclosed(neighbors, plan, slots, groups, width):
    fanout = neighbors.shape[0]
    lists = jnp.transpose(neighbors.reshape(fanout, slots, -1, width), (1, 2, 0, 3))
    lists = jnp.pad(lists, ((0, 0), (0, 0), (0, 2 * LIST_ROWS - fanout), (0, 0)))
    letters = jnp.concatenate([lists // 32, lists % 32], axis=1).reshape(slots, groups, LIST_ROWS, width)
    note = jnp.broadcast_to(jnp.pad(plan, (0, width - plan.shape[0])), (slots, groups, 2, width))
    return jnp.concatenate([letters, note], axis=2).astype(jnp.bfloat16)


def permute_kernel(x_ref, source_ref, out_ref):
    rows = x_ref.shape[0]
    positions = lax.broadcasted_iota(jnp.int32, (TILE, rows), 1)
    for tile in range(rows // TILE):
        own = slice(tile * TILE, (tile + 1) * TILE)
        chosen = jnp.where(positions == source_ref[own, :], 1.0, 0.0).astype(jnp.bfloat16)
        out_ref[own, :] = jnp.dot(chosen, x_ref[...], preferred_element_type=jnp.float32).astype(jnp.bfloat16)


def permute_rows(x, source):
    vmem = pl.BlockSpec(memory_space=pltpu.VMEM)
    return pl.pallas_call(
        permute_kernel,
        out_shape=jax.ShapeDtypeStruct(x.shape, x.dtype),
        in_specs=[vmem, vmem],
        out_specs=vmem,
        compiler_params=pltpu.CompilerParams(vmem_limit_bytes=16 << 20),
        cost_estimate=pl.CostEstimate(flops=1_100_000_000, bytes_accessed=2_100_000, transcendentals=0),
        name="permute",
    )(x, source.reshape(-1, 1))


def regroup_kernel(x_ref, out_ref, places_ref, joined):
    pieces = x_ref.shape[0]
    rows, width = joined.shape
    body = SIDE * width // LANES
    for i in range(pieces):
        for c in range(width // LANES):
            joined[i * SIDE : (i + 1) * SIDE, c * LANES : (c + 1) * LANES] = x_ref[i, c * SIDE : (c + 1) * SIDE, :]
    high, low = [], []
    for i in range(0, pieces, LANES // SIDE):
        notes = [x_ref[i + k, body:, :].astype(jnp.float32) for k in range(LANES // SIDE)]
        note = functools.reduce(jnp.add, notes)
        high.append(note[0:1, :])
        low.append(note[1:2, :])
    places = (jnp.concatenate(high, axis=1) * 32.0 + jnp.concatenate(low, axis=1)).astype(jnp.int32)
    places_ref[...] = jnp.broadcast_to(places, places_ref.shape)
    for tile in range(rows // TILE):
        own = lax.broadcasted_iota(jnp.int32, (TILE, rows), 0) + tile * TILE
        chosen = jnp.where(own == places, 1.0, 0.0).astype(jnp.bfloat16)
        out_ref[tile * TILE : (tile + 1) * TILE, :] = jnp.dot(
            chosen, joined[...], preferred_element_type=jnp.float32
        ).astype(jnp.bfloat16)


def regroup_rows(x, rows, width):
    vmem = pl.BlockSpec(memory_space=pltpu.VMEM)
    return pl.pallas_call(
        regroup_kernel,
        out_shape=(jax.ShapeDtypeStruct((rows, width), x.dtype), jax.ShapeDtypeStruct((8, rows), jnp.int32)),
        in_specs=[vmem],
        out_specs=(vmem, vmem),
        scratch_shapes=[pltpu.VMEM((rows, width), jnp.bfloat16)],
        compiler_params=pltpu.CompilerParams(vmem_limit_bytes=16 << 20),
        cost_estimate=pl.CostEstimate(flops=1_100_000_000, bytes_accessed=2_200_000, transcendentals=0),
        name="regroup",
    )(x)


def pick_kernel(source_ref, x_ref, out_ref):
    for q in range(out_ref.shape[0]):
        out_ref[q] = x_ref[source_ref[q]]


def pick_parts(x, source):
    vmem = pl.BlockSpec(memory_space=pltpu.VMEM)
    return pl.pallas_call(
        pick_kernel,
        out_shape=jax.ShapeDtypeStruct((source.shape[0],) + x.shape[1:], x.dtype),
        in_specs=[pl.BlockSpec(memory_space=pltpu.SMEM), vmem],
        out_specs=vmem,
        compiler_params=pltpu.CompilerParams(vmem_limit_bytes=16 << 20),
        cost_estimate=pl.CostEstimate(flops=0, bytes_accessed=2_300_000, transcendentals=0),
        name="pick",
    )(source, x)


def homeward_kernel(owner_ref, live_ref, x_ref, out_ref):
    groups, slots, part, width = out_ref.shape
    quarter = part // SIDE
    row = lax.broadcasted_iota(jnp.int32, (part, part), 0)
    column = lax.broadcasted_iota(jnp.int32, (part, part), 1)
    order = jnp.where(column == (row % SIDE) * quarter + row // SIDE, 1.0, 0.0).astype(jnp.bfloat16)
    for g in range(groups):
        for s in range(slots):
            start = pl.multiple_of(owner_ref[g * slots + s] * part, part)
            piece = jnp.dot(order, x_ref[pl.ds(start, part), :], preferred_element_type=jnp.float32)
            keep = live_ref[g * slots + s] > 0
            out_ref[g, s] = jnp.where(keep, piece, 0.0).astype(jnp.bfloat16)


def homeward_parts(x, owner, live, groups, slots):
    rows, width = x.shape
    smem = pl.BlockSpec(memory_space=pltpu.SMEM)
    vmem = pl.BlockSpec(memory_space=pltpu.VMEM)
    return pl.pallas_call(
        homeward_kernel,
        out_shape=jax.ShapeDtypeStruct((groups, slots, rows // groups, width), x.dtype),
        in_specs=[smem, smem, vmem],
        out_specs=vmem,
        compiler_params=pltpu.CompilerParams(vmem_limit_bytes=16 << 20),
        cost_estimate=pl.CostEstimate(flops=270_000_000, bytes_accessed=3_200_000, transcendentals=0),
        name="homeward",
    )(owner, live, x)


def exchange(x, axis):
    return lax.all_to_all(x, axis, split_axis=0, concat_axis=0, tiled=True)


def body(
    home_points,
    counts,
    owner_group,
    neighbors_home,
    hilbert_target,
    neighbors_second,
    depth_first,
    mixing_first,
    gain_first,
    w_qkv_first,
    w_out_first,
    depth_second,
    mixing_second,
    gain_second,
    w_qkv_second,
    w_out_second,
):
    groups = lax.axis_size("grp")
    owners = lax.axis_size("dev")
    home_rows, width = home_points.shape
    slots = owner_group.shape[0]
    rows = home_rows // slots
    blocks = hilbert_target.shape[0]
    part = rows // groups
    side = rows // owners
    first_params = (depth_first, mixing_first, gain_first, w_qkv_first, w_out_first)
    second_params = (depth_second, mixing_second, gain_second, w_qkv_second, w_out_second)

    letters = enclosed(neighbors_home, jnp.concatenate([counts, owner_group]), slots, groups, width)
    points = jnp.concatenate([home_points.reshape(slots, groups, part, width), letters], axis=2)
    spread = exchange(jnp.transpose(points, (1, 0, 2, 3)), "grp")
    plan = spread[:, 0, part + LIST_ROWS, : 1 + slots].astype(jnp.int32)
    live = (jnp.arange(slots)[None, :] < plan[:, :1]).reshape(-1)
    owner = plan[:, 1:].reshape(-1)
    match = live[None, :] & (owner[None, :] == jnp.arange(groups)[:, None])
    source = jnp.sum(jnp.where(match, jnp.arange(groups * slots)[None, :], 0), axis=1)
    owned = exchange(pick_parts(spread.reshape((groups * slots,) + spread.shape[2:]), source), "grp")

    arrival = (neighbors_second % side) * side + neighbors_second // side
    second_lists = staged(arrival, rows)
    column = lax.axis_index("dev")
    pair = jnp.arange(2)[None, :]
    places = (2 * hilbert_target[:, None] + pair).reshape(1, -1)
    digits = jnp.concatenate([places // 32, places % 32, jnp.zeros((NOTE_ROWS - 2, side), jnp.int32)])
    mine = jnp.arange(LANES // side) == column % (LANES // side)
    note = jnp.where(mine[None, :, None], digits[:, None, :], 0).reshape(NOTE_ROWS, LANES).astype(jnp.bfloat16)

    section_one = encoder_block(owned, note, first_params, rows, True)
    mid, places = regroup_rows(exchange(section_one, "dev"), rows, width)
    targets = places[0].reshape(owners, blocks, 2)[:, :, 0] // 2
    by_part = jnp.transpose(targets.reshape(owners, groups, -1), (1, 0, 2)).reshape(-1, 1)
    backward_rows = (2 * by_part + pair).reshape(-1)
    regrouped = exchange(mid.reshape(owners, side, width), "dev").reshape(rows, width)
    section_two = encoder_block(regrouped, second_lists, second_params, rows, False)
    mid = exchange(section_two.reshape(owners, side, width), "dev").reshape(rows, width)
    mid = permute_rows(mid, backward_rows)
    returned = exchange(mid.reshape(groups * owners, -1, width), ("grp", "dev")).reshape(rows, width)
    homeward = homeward_parts(returned, owner, live.astype(jnp.int32), groups, slots)
    delivered = exchange(homeward, "grp")
    return jnp.transpose(delivered, (1, 0, 2, 3)).reshape(home_rows, width)


def solution(mesh):
    return jax.shard_map(
        body,
        mesh=mesh,
        in_specs=(
            P(("grp", "dev"), None),
            P(("grp", "dev")),
            P(("grp", "dev")),
            P(None, ("grp", "dev")),
            P(("grp", "dev")),
            P(None, ("grp", "dev")),
            P(),
            P(),
            P(),
            P(),
            P(),
            P(),
            P(),
            P(),
            P(),
            P(),
        ),
        out_specs=P(("grp", "dev"), None),
        check_vma=False,
    )
```
